32 devices in a mesh: layer: 2 (over y), feat: 16 (over z, x, core).
Axes of the slice: x: 2, y: 2, z: 4, core: 2. Of those that a mesh axis runs over, the one named last changes fastest.
Arguments:
- residual: bfloat16 [2, 256, 4096], P('layer', 'feat'), may hold values from -6 to 6
- targets: bfloat16 [2, 256, 4096], P('layer', 'feat'), may hold values from -6 to 6
- w_enc: bfloat16 [2, 4096, 8192], P('layer', None, 'feat'), may hold values from -0.09375 to 0.09375
- b_enc: float32 [2, 8192], P('layer', 'feat'), may hold values from -3 to 3
- w_dec: bfloat16 [2, 8192, 4096], P('layer', 'feat'), may hold values from -0.0625 to 0.0625
- block_mask: int32 [2, 2, 64], P('layer', None, 'feat'), may hold values from 0 to 1, as said below
Outputs:
- grad_encoder: bfloat16 [2, 4096, 8192], P('layer', None, 'feat')
- grad_bias: float32 [2, 8192], P('layer', 'feat')
- grad_decoder: bfloat16 [2, 8192, 4096], P('layer', 'feat')
- loss: float32 [], replicated
The draws below stay inside these ranges and needn't reach their ends.
Inputs may be any that keep to these rules, and one draw needn't show every extreme that they name: `block_mask`: each feature block of a layer has its own activity level, so the number of active blocks differs from device to device; some feature blocks are never active and some always.
All inputs are finite; a program needn't handle non-finite values.
Results may differ from the reference program's by a relative error of at most 0.0056.
Values may be sent and summed in bfloat16 or wider, within the bound.
No kernel may reach another device: no remote copies, remote signals or barrier semaphores. Data moves between devices by JAX's collectives and lax.ppermute only.
A program may use at most 64 MiB of HBM per device.

```python
import jax
import jax.numpy as jnp
from jax import lax

D = 4096
F = 8192
TOKENS = 256
TBLOCK = 128
FBLOCK = 128
LAYERS = 2


def draw_block_mask(key, part):
    level_key, roll_key = jax.random.split(key)
    levels = jax.random.randint(level_key, (LAYERS, 1, F // FBLOCK), 0, 5)
    rolls = jax.random.randint(roll_key, (LAYERS, TOKENS // TBLOCK, F // FBLOCK), 0, 4)
    return (rolls < levels).astype(jnp.int32)


def level_of(own_key, extent, shards, low, high):
    level = 1.0
    for axis_at, shards_of in shards:
        draws = jax.random.uniform(jax.random.fold_in(jax.random.fold_in(own_key, 6), axis_at), (shards_of,), jnp.float32, low / len(shards), high / len(shards))
        level = level * jnp.repeat(jnp.exp(draws), extent[axis_at] // shards_of).reshape((-1,) + (1,) * (len(extent) - 1 - axis_at))
    return level


def gaussian(rng, shape, spread, reach, cuts=(), held_as=jnp.bfloat16):
    entries = spread * jax.random.normal(rng, shape, jnp.float32)
    if cuts:
        entries = entries * level_of(rng, shape, cuts, -0.22, 0.18)
    return jnp.clip(entries, -reach, reach).astype(held_as)


def setup_inputs(seed: int = 0) -> dict:
    key_list = jax.random.split(jax.random.key(seed), 7)
    return {
        "residual": gaussian(key_list[0], (LAYERS, TOKENS, D), 1.0, 6.0, ((0, 2), (1, 16))),
        "targets": gaussian(key_list[1], (LAYERS, TOKENS, D), 1.0, 6.0, ((0, 2), (1, 16))),
        "w_enc": gaussian(key_list[2], (LAYERS, D, F), D ** -0.5, 0.09375, ((0, 2), (2, 16))),
        "b_enc": gaussian(key_list[3], (LAYERS, F), 0.5, 3.0, ((0, 2), (1, 16)), jnp.float32),
        "w_dec": gaussian(key_list[4], (LAYERS, F, D), F ** -0.5, 0.0625, ((0, 2), (1, 16))),
        "block_mask": draw_block_mask(jax.random.fold_in(key_list[6], 71), 0),
    }


penalty_weight = 0.5
norm_epsilon = 1e-06

def expand_mask(blocks):
    return jnp.repeat(jnp.repeat(blocks, TBLOCK, axis=0), FBLOCK, axis=1).astype(jnp.float32)

def reference(residual, targets, w_enc, b_enc, w_dec, block_mask):
    layers = residual.shape[0]
    activations = []
    positives = []
    keep_masks = []
    row_norms = []
    for layer in range(layers):
        preact = jnp.dot(residual[layer], w_enc[layer], preferred_element_type=jnp.float32) + b_enc[layer]
        positive = jnp.maximum(preact, 0.0)
        keep_mask = expand_mask(block_mask[layer])
        activations.append((keep_mask * positive * positive).astype(jnp.bfloat16))
        positives.append(positive)
        keep_masks.append(keep_mask)
        row_norms.append(jnp.sqrt(lax.optimization_barrier(jnp.sum(jnp.square(w_dec[layer].astype(jnp.float32)), axis=1)) + norm_epsilon))
    misfits = []
    square_sum = jnp.zeros((), jnp.float32)
    penalty_sum = jnp.zeros((), jnp.float32)
    for target in range(layers):
        source = (target - 1) % layers
        recon = jnp.dot(activations[source], w_dec[source], preferred_element_type=jnp.float32)
        misfit = recon - targets[target].astype(jnp.float32)
        misfits.append(misfit)
        square_sum = square_sum + jnp.sum(misfit * misfit)
    enc_grads = []
    bias_grads = []
    dec_grads = []
    for layer in range(layers):
        activation = activations[layer]
        act_float = activation.astype(jnp.float32)
        penalty_sum = penalty_sum + jnp.sum(act_float * row_norms[layer][None, :])
        error_back = misfits[(layer + 1) % layers].astype(jnp.bfloat16)
        decoder = w_dec[layer]
        dec_grad = jnp.dot(activation.T, error_back, preferred_element_type=jnp.float32)
        act_sum = lax.optimization_barrier(jnp.sum(act_float, axis=0))
        dec_grad = dec_grad + penalty_weight * act_sum[:, None] * decoder.astype(jnp.float32) / row_norms[layer][:, None]
        dec_grads.append(dec_grad.astype(jnp.bfloat16))
        act_grad = jnp.dot(error_back, decoder.T, preferred_element_type=jnp.float32)
        act_grad = act_grad + penalty_weight * row_norms[layer][None, :]
        pre_grad = (act_grad * keep_masks[layer] * 2.0 * positives[layer]).astype(jnp.bfloat16)
        bias_grads.append(lax.optimization_barrier(jnp.sum(pre_grad.astype(jnp.float32), axis=0)))
        enc_grads.append(jnp.dot(residual[layer].T, pre_grad, preferred_element_type=jnp.float32).astype(jnp.bfloat16))
    loss = (0.5 * square_sum + penalty_weight * penalty_sum) / (layers * TOKENS * D)
    return (jnp.stack(enc_grads), jnp.stack(bias_grads), jnp.stack(dec_grads), loss)
```

```python
import jax
import jax.numpy as jnp
import numpy as np
from jax import lax
from jax.sharding import PartitionSpec as P

TBLOCK = 128
FBLOCK = 128
PAD = 128

penalty_weight = 0.5
norm_epsilon = 1e-06
f32 = jnp.float32
bf16 = jnp.bfloat16


class Ring:
    def __init__(self, size):
        self.size = size
        chips = size // 2
        self.chips = chips
        self.hops = (chips - 1) // 2
        self.far = chips % 2 == 0
        order = list(range(0, chips, 2)) + list(range(1, chips, 2))[::-1]
        place = {chip: at for at, chip in enumerate(order)}
        self.step, self.far_step = [], []
        owners = []
        for device in range(size):
            chip, core = divmod(device, 2)
            at = place[chip]
            ahead = 1 if core == 0 else -1
            pair = (device, order[(at + ahead) % chips] * 2 + core)
            self.step.append(pair)
            if core == 1:
                self.far_step.append(pair)
            behind = [order[(at - ahead * k) % chips] for k in range(1, self.hops + 1)]
            front = [order[(at + ahead * k) % chips] for k in range(1, self.hops + 1)]
            last = [order[(at + self.hops + 1) % chips]] if self.far else []
            owners.append([2 * c + i for c in [chip] + behind + front + last for i in (0, 1)])
        self.owners = np.array(owners, np.int32)
        self.twin = [(device, device ^ 1) for device in range(size)]

    def along(self, block):
        return lax.ppermute(block, "feat", self.step)

    def along_far(self, block):
        return lax.ppermute(block, "feat", self.far_step)

    def across(self, block):
        return lax.ppermute(block, "feat", self.twin)


def chip_block(ring, core, own):
    other = ring.across(own)
    return jnp.concatenate(
        [jnp.where(core == 0, own, other), jnp.where(core == 0, other, own)], axis=0
    )


def gather(ring, core, block):
    behind = []
    moving = block
    for _ in range(ring.hops):
        moving = ring.along(moving)
        behind.append(moving)
    parts = [block] + behind
    if behind:
        parts.append(ring.across(jnp.concatenate(behind, axis=0)))
    if ring.far:
        came = ring.along_far(moving)
        parts.append(jnp.where(core == 1, came, ring.across(came)))
    return jnp.concatenate(parts, axis=0)


def scatter_sum(ring, rows, partial):
    sent = partial.astype(bf16)
    at = rows * (1 + ring.hops)
    end = rows * (1 + 2 * ring.hops)
    arrived = None
    if ring.far:
        total = partial[end:] + ring.across(sent[end:]).astype(f32)
        arrived = ring.along_far(total.astype(bf16))
    if ring.hops:
        from_twin = ring.across(sent[rows:at])
    for k in range(ring.hops, 0, -1):
        total = partial[at + rows * (k - 1) : at + rows * k]
        total = total + from_twin[rows * (k - 1) : rows * k].astype(f32)
        if arrived is not None:
            total = total + arrived.astype(f32)
        arrived = ring.along(total.astype(bf16))
    total = partial[:rows]
    if arrived is not None:
        total = total + arrived.astype(f32)
    mine = total.astype(bf16)
    return mine.astype(f32) + ring.across(mine).astype(f32)


def contract_rows(left, right):
    return lax.dot_general(
        left, right, (((0,), (0,)), ((), ())), preferred_element_type=f32
    )


def split_three(value):
    high = value.astype(bf16)
    rest = value - high.astype(f32)
    middle = rest.astype(bf16)
    low = (rest - middle.astype(f32)).astype(bf16)
    return [high, middle, low]


def body(residual, targets, w_enc, b_enc, w_dec, block_mask):
    encoder = w_enc[0]
    enc_bias = b_enc[0]
    decoder = w_dec[0]
    blocks = block_mask[0].astype(f32)
    row_count = residual.shape[1]
    width = residual.shape[2]
    layers = lax.axis_size("layer")
    feats = lax.axis_size("feat")
    tokens = row_count * feats
    ring = Ring(feats)
    device = lax.axis_index("feat")
    core = device % 2
    halves = 2 if row_count % 2 == 0 else 1
    rows = row_count // halves
    block_rows = 2 * rows

    goal = lax.ppermute(
        targets[0], "layer", [(i, (i - 1) % layers) for i in range(layers)]
    )
    owner = jnp.asarray(ring.owners)[device]
    mask_columns = jnp.repeat(blocks, FBLOCK, axis=1)

    row_norms = jnp.sqrt(jnp.sum(jnp.square(decoder.astype(f32)), axis=1) + norm_epsilon)

    own_block = chip_block(ring, core, residual[0])
    goal_block = chip_block(ring, core, goal)

    def half_of(block, h):
        return jnp.concatenate(
            [block[c * row_count + h * rows : c * row_count + (h + 1) * rows] for c in (0, 1)], axis=0
        )

    gathered = [gather(ring, core, half_of(own_block, h)) for h in range(halves)]
    keep, positive, activation, penalty = [], [], [], jnp.zeros((), f32)
    for h in range(halves):
        token = (owner[:, None] * row_count + h * rows + jnp.arange(rows)[None, :]).reshape(-1)
        token_block = token // TBLOCK
        mask = jnp.zeros((token.shape[0], mask_columns.shape[1]), f32)
        for b in range(blocks.shape[0]):
            mask = jnp.where((token_block == b)[:, None], mask_columns[b][None, :], mask)
        preact = jnp.dot(gathered[h], encoder, preferred_element_type=f32) + enc_bias
        positive.append(jnp.maximum(preact, 0.0))
        keep.append(mask)
        activation.append((mask * positive[h] * positive[h]).astype(bf16))
        penalty = penalty + jnp.sum(activation[h].astype(f32) * row_norms[None, :])
    penalty_chip = penalty + ring.across(penalty)
    errors, losses = [], []
    for h in range(halves):
        partial = jnp.dot(activation[h], decoder, preferred_element_type=f32)
        recon = scatter_sum(ring, block_rows, partial)
        misfit = recon - half_of(goal_block, h).astype(f32)
        loss_part = 0.5 * jnp.sum(misfit * misfit)
        if h == halves - 1:
            loss_part = loss_part + penalty_weight * penalty_chip
        three = jnp.stack(split_three(loss_part))
        tail = jnp.broadcast_to(jnp.pad(three, (0, PAD - 3))[None, :], (block_rows, PAD))
        payload = jnp.concatenate([misfit.astype(bf16), tail], axis=1)
        every = gather(ring, core, payload)
        errors.append(every[:, :width])
        losses.append(jnp.sum(every[::block_rows, width : width + 3].astype(f32)))
    loss_sum = sum(losses)
    whole = loss_sum
    for _ in range(layers - 1):
        loss_sum = lax.ppermute(
            loss_sum, "layer", [(i, (i + 1) % layers) for i in range(layers)]
        )
        whole = whole + loss_sum
    loss = whole / (layers * tokens * width)

    all_errors = jnp.concatenate(errors, axis=0)
    all_act = jnp.concatenate(activation, axis=0)
    all_rows = jnp.concatenate(gathered, axis=0)
    act_sum = jnp.sum(all_act.astype(f32), axis=0)
    dec_grad = (
        contract_rows(all_act, all_errors)
        + penalty_weight * act_sum[:, None] * decoder.astype(f32) / row_norms[:, None]
    )
    pre_grads = []
    for h in range(halves):
        act_grad = lax.dot_general(
            errors[h], decoder, (((1,), (1,)), ((), ())), preferred_element_type=f32
        )
        act_grad = act_grad + penalty_weight * row_norms[None, :]
        pre_grads.append((act_grad * keep[h] * 2.0 * positive[h]).astype(bf16))
    pre_grad = jnp.concatenate(pre_grads, axis=0)
    bias_grad = jnp.sum(pre_grad.astype(f32), axis=0)
    enc_grad = contract_rows(all_rows, pre_grad)
    return (
        enc_grad.astype(bf16)[None],
        bias_grad[None],
        dec_grad.astype(bf16)[None],
        loss,
    )


def solution(mesh):
    return jax.shard_map(
        body,
        mesh=mesh,
        in_specs=(
            P("layer", "feat", None),
            P("layer", "feat", None),
            P("layer", None, "feat"),
            P("layer", "feat"),
            P("layer", "feat", None),
            P("layer", None, "feat"),
        ),
        out_specs=(P("layer", None, "feat"), P("layer", "feat"), P("layer", "feat", None), P()),
        check_vma=False,
    )
```

```python
import functools

import jax
import jax.numpy as jnp
import numpy as np
from jax import lax
from jax.experimental import pallas as pl
from jax.experimental.pallas import tpu as pltpu
from jax.sharding import PartitionSpec as P

TBLOCK = 128
FBLOCK = 128
PAD = 128

penalty_weight = 0.5
norm_epsilon = 1e-06
f32 = jnp.float32
bf16 = jnp.bfloat16


class Ring:
    def __init__(self, size):
        self.size = size
        chips = size // 2
        self.chips = chips
        self.hops = (chips - 1) // 2
        self.far = chips % 2 == 0
        order = list(range(0, chips, 2)) + list(range(1, chips, 2))[::-1]
        place = {chip: at for at, chip in enumerate(order)}
        self.step, self.far_step = [], []
        owners = []
        for device in range(size):
            chip, core = divmod(device, 2)
            at = place[chip]
            ahead = 1 if core == 0 else -1
            pair = (device, order[(at + ahead) % chips] * 2 + core)
            self.step.append(pair)
            if core == 1:
                self.far_step.append(pair)
            behind = [order[(at - ahead * k) % chips] for k in range(1, self.hops + 1)]
            front = [order[(at + ahead * k) % chips] for k in range(1, self.hops + 1)]
            last = [order[(at + self.hops + 1) % chips]] if self.far else []
            owners.append([2 * c + i for c in [chip] + behind + front + last for i in (0, 1)])
        self.owners = np.array(owners, np.int32)
        self.twin = [(device, device ^ 1) for device in range(size)]

    def along(self, block):
        return lax.ppermute(block, "feat", self.step)

    def along_far(self, block):
        return lax.ppermute(block, "feat", self.far_step)

    def across(self, block):
        return lax.ppermute(block, "feat", self.twin)


def chip_block(ring, core, own):
    other = ring.across(own)
    return jnp.concatenate(
        [jnp.where(core == 0, own, other), jnp.where(core == 0, other, own)], axis=0
    )


def after(values, signal):
    return lax.optimization_barrier((values, signal))[0]


def gather(ring, core, block):
    behind = []
    moving = block
    for _ in range(ring.hops):
        moving = ring.along(moving)
        behind.append(moving)
    parts = [block]
    came = None
    if ring.far:
        came = ring.along_far(moving)
    if behind:
        stack = jnp.concatenate(behind, axis=0)
        parts += [stack, ring.across(stack)]
    if ring.far:
        parts.append(jnp.where(core == 1, came, ring.across(came)))
    return parts, behind


def scatter_sum(ring, rows, own, sent, front, last):
    from_twin = ring.across(sent)
    arrived = None
    states = []
    if ring.far:
        total = last + from_twin[rows * ring.hops :].astype(f32)
        arrived = ring.along_far(total.astype(bf16))
    for k in range(ring.hops, 0, -1):
        total = front[rows * (k - 1) : rows * k]
        total = total + from_twin[rows * (k - 1) : rows * k].astype(f32)
        if arrived is not None:
            total = total + arrived.astype(f32)
        arrived = ring.along(total.astype(bf16))
        states.append(arrived)
    total = own
    if arrived is not None:
        total = total + arrived.astype(f32)
    mine = total.astype(bf16)
    return mine.astype(f32) + ring.across(mine).astype(f32), states


def in_vmem(x):
    return pltpu.with_memory_space_constraint(x, pltpu.VMEM)


VMEM_SPEC = pl.BlockSpec(memory_space=pltpu.VMEM)
ANY_SPEC = pl.BlockSpec(memory_space=pl.ANY)


def stacked(refs, columns):
    return jnp.concatenate([ref[:, columns] for ref in refs], axis=0)


def whole_pieces(parts):
    if all(p.shape[0] % 16 == 0 for p in parts):
        return parts
    return [jnp.concatenate(parts, axis=0)]


def forward_kernel(count, step, *refs):
    pieces = refs[:count]
    enc_ref, bias_ref, keep_ref, dec_ref = refs[count : count + 4]
    act_ref, gate_ref, sum_ref = refs[count + 4 : count + 7]
    outs = refs[count + 7 :]
    width = dec_ref.shape[1]
    preact = jnp.zeros(gate_ref.shape, f32)
    for at in range(0, width, step):
        preact = preact + jnp.dot(
            stacked(pieces, slice(at, at + step)), enc_ref[at : at + step, :], preferred_element_type=f32
        )
    positive = jnp.maximum(preact + bias_ref[...], 0.0)
    keep = keep_ref[...]
    act = (keep * positive * positive).astype(bf16)
    act_ref[...] = act
    gate_ref[...] = keep * 2.0 * positive
    sum_ref[...] = jnp.sum(act.astype(f32), axis=0, keepdims=True)
    for at in range(0, width, step):
        part = jnp.dot(act, dec_ref[:, at : at + step], preferred_element_type=f32)
        if len(outs) == 1:
            outs[0][:, at : at + step] = part
            continue
        own_ref, sent_ref, front_ref, last_ref = outs
        rows, hop = own_ref.shape[0], front_ref.shape[0]
        own_ref[:, at : at + step] = part[:rows]
        sent_ref[:hop, at : at + step] = part[rows : rows + hop].astype(bf16)
        sent_ref[hop:, at : at + step] = part[rows + 2 * hop :].astype(bf16)
        front_ref[:, at : at + step] = part[rows + hop : rows + 2 * hop]
        last_ref[:, at : at + step] = part[rows + 2 * hop :]


def forward(parts, encoder, bias, keep, decoder):
    pieces = whole_pieces(parts)
    total, features = keep.shape
    width = decoder.shape[1]
    shapes = [((total, features), bf16), ((total, features), f32), ((1, features), f32)]
    if len(pieces) == 4:
        rows, hop = parts[0].shape[0], parts[1].shape[0]
        shapes += [((rows, width), f32), ((hop + rows, width), bf16), ((hop, width), f32), ((rows, width), f32)]
    else:
        shapes += [((total, width), f32)]
    flops = 4 * total * features * width
    outs = pl.pallas_call(
        functools.partial(forward_kernel, len(pieces), min(512, width)),
        out_shape=[pltpu.VMEM(shape, dtype) for shape, dtype in shapes],
        in_specs=[VMEM_SPEC] * (len(pieces) + 4),
        out_specs=[VMEM_SPEC] * len(shapes),
        compiler_params=pltpu.CompilerParams(vmem_limit_bytes=12 << 20),
        cost_estimate=pl.CostEstimate(flops=flops, bytes_accessed=1 << 20, transcendentals=0),
    )(*[in_vmem(x) for x in (*pieces, encoder, bias, keep, decoder)])
    act, gate, act_sum = outs[:3]
    if len(outs) > 4:
        return act, gate, act_sum, outs[3:]
    full = outs[3]
    sizes = [p.shape[0] for p in parts]
    ends = np.cumsum([0] + sizes)
    cut = [full[ends[i] : ends[i + 1]] for i in range(len(sizes))]
    own = cut[0]
    hop = sizes[1] if len(sizes) > 2 else 0
    front = full[ends[2] : ends[3]] if hop else None
    last = cut[-1] if len(sizes) % 2 == 0 else full[:0]
    behind = full[ends[1] : ends[2]] if hop else full[:0]
    sent = jnp.concatenate([behind, last], axis=0).astype(bf16)
    return act, gate, act_sum, (own, sent, front, last)


def turn_kernel(*refs):
    pieces, out_ref = refs[:-1], refs[-1]
    step = 128 if out_ref.shape[0] % 128 == 0 else out_ref.shape[0]
    for at in range(0, out_ref.shape[0], step):
        out_ref[at : at + step, :] = stacked(pieces, slice(at, at + step)).T


def turned(parts):
    pieces = whole_pieces(parts)
    total = sum(p.shape[0] for p in pieces)
    width = pieces[0].shape[1]
    return pl.pallas_call(
        turn_kernel,
        out_shape=pltpu.VMEM((width, total), bf16),
        in_specs=[VMEM_SPEC] * len(pieces),
        out_specs=VMEM_SPEC,
        compiler_params=pltpu.CompilerParams(vmem_limit_bytes=12 << 20),
        cost_estimate=pl.CostEstimate(flops=0, bytes_accessed=4 << 20, transcendentals=0),
    )(*[in_vmem(x) for x in pieces])


def backward_kernel(counts, step, *refs):
    halves = len(counts)
    at = sum(counts)
    errors = refs[:at]
    acts, gates, rows = (refs[at + halves * i : at + halves * (i + 1)] for i in range(3))
    dec_ref, norm_ref, coef_ref = refs[at + 3 * halves : at + 3 * halves + 3]
    enc_out, bias_out, dec_out = refs[at + 3 * halves + 3 : at + 3 * halves + 6]
    enc_stage, dec_stage, enc_sems, dec_sems = refs[at + 3 * halves + 6 :]
    features, width = dec_ref.shape
    turned_act = jnp.concatenate([a[...] for a in acts], axis=0).T
    coef = coef_ref[...]
    copies = []
    for i, at in enumerate(range(0, width, step)):
        columns = slice(at, at + step)
        grad = jnp.dot(turned_act, stacked(errors, columns), preferred_element_type=f32)
        grad = grad + coef * dec_ref[:, columns].astype(f32)
        dec_stage[:, columns] = grad.astype(bf16)
        copy = pltpu.make_async_copy(dec_stage.at[:, columns], dec_out.at[:, columns], dec_sems.at[i])
        copy.start()
        copies.append(copy)
    total = turned_act.shape[1]
    act_grad = jnp.zeros((total, features), f32)
    for at in range(0, width, step):
        columns = slice(at, at + step)
        act_grad = act_grad + lax.dot_general(
            stacked(errors, columns), dec_ref[:, columns], (((1,), (1,)), ((), ())), preferred_element_type=f32
        )
    gate = jnp.concatenate([g[...] for g in gates], axis=0)
    pre_grad = ((act_grad + penalty_weight * norm_ref[...]) * gate).astype(bf16)
    bias_out[...] = jnp.sum(pre_grad.astype(f32), axis=0, keepdims=True)
    for i, at in enumerate(range(0, width, step)):
        here = slice(at, at + step)
        left = jnp.concatenate([r[here, :] for r in rows], axis=1)
        enc_stage[here, :] = jnp.dot(left, pre_grad, preferred_element_type=f32).astype(bf16)
        copy = pltpu.make_async_copy(enc_stage.at[here, :], enc_out.at[here, :], enc_sems.at[i])
        copy.start()
        copies.append(copy)
    for copy in copies:
        copy.wait()


def backward(errors, acts, gates, rows, decoder, norms, coef):
    errors = [whole_pieces(e) for e in errors]
    features, width = decoder.shape
    step = min(512, width)
    operands = [x for e in errors for x in e] + acts + gates + rows + [decoder, norms, coef]
    total = sum(a.shape[0] for a in acts)
    return pl.pallas_call(
        functools.partial(backward_kernel, tuple(len(e) for e in errors), step),
        out_shape=[
            jax.ShapeDtypeStruct((width, features), bf16),
            jax.ShapeDtypeStruct((1, features), f32),
            jax.ShapeDtypeStruct((features, width), bf16),
        ],
        in_specs=[VMEM_SPEC] * len(operands),
        out_specs=[ANY_SPEC, VMEM_SPEC, ANY_SPEC],
        scratch_shapes=[
            pltpu.VMEM((width, features), bf16),
            pltpu.VMEM((features, width), bf16),
            pltpu.SemaphoreType.DMA((width // step,)),
            pltpu.SemaphoreType.DMA((width // step,)),
        ],
        compiler_params=pltpu.CompilerParams(vmem_limit_bytes=24 << 20),
        cost_estimate=pl.CostEstimate(flops=6 * total * features * width, bytes_accessed=8 << 20, transcendentals=0),
    )(*[in_vmem(x) for x in operands])


def split_three(value):
    high = value.astype(bf16)
    rest = value - high.astype(f32)
    middle = rest.astype(bf16)
    low = (rest - middle.astype(f32)).astype(bf16)
    return [high, middle, low]


def body(residual, targets, w_enc, b_enc, w_dec, block_mask):
    row_count = residual.shape[1]
    width = residual.shape[2]
    layers = lax.axis_size("layer")
    feats = lax.axis_size("feat")
    tokens = row_count * feats
    ring = Ring(feats)
    device = lax.axis_index("feat")
    core = device % 2
    halves = 2 if row_count % 16 == 0 else 1
    rows = row_count // halves
    block_rows = 2 * rows

    def half_of(block, h):
        return jnp.concatenate(
            [block[c * row_count + h * rows : c * row_count + (h + 1) * rows] for c in (0, 1)], axis=0
        )

    own_block = chip_block(ring, core, residual[0])
    gathered, steps = [], []
    for h in range(halves):
        parts, behind = gather(ring, core, half_of(own_block, h))
        gathered.append(parts)
        steps.append(behind)
    first = steps[0][0]
    targets, b_enc, w_dec_later, block_mask = after((targets, b_enc, w_dec, block_mask), first)

    goal = lax.ppermute(targets[0], "layer", [(i, (i - 1) % layers) for i in range(layers)])
    goal_block = chip_block(ring, core, goal)
    row_norms = jnp.sqrt(jnp.sum(jnp.square(w_dec_later[0].astype(f32)), axis=1) + norm_epsilon)
    owner = jnp.asarray(ring.owners)[device]
    mask_columns = jnp.repeat(block_mask[0].astype(f32), FBLOCK, axis=1)
    encoder = w_enc[0]
    decoder = w_dec[0]
    bias = b_enc[0][None, :]

    acts, gates, shares, act_sum = [], [], [], None
    for h in range(halves):
        token = (owner[:, None] * row_count + h * rows + jnp.arange(rows)[None, :]).reshape(-1)
        token_block = token // TBLOCK
        keep = jnp.zeros((token.shape[0], mask_columns.shape[1]), f32)
        for b in range(mask_columns.shape[0]):
            keep = jnp.where((token_block == b)[:, None], mask_columns[b][None, :], keep)
        act, gate, half_sum, share = forward(gathered[h], encoder, bias, keep, decoder)
        acts.append(act)
        gates.append(gate)
        shares.append(share)
        act_sum = half_sum if act_sum is None else act_sum + half_sum
    act_sum = act_sum[0]
    penalty = jnp.sum(act_sum * row_norms)
    penalty_chip = penalty + ring.across(penalty)
    errors, turned_rows = [], []
    loss_part = penalty_weight * penalty_chip
    for h in range(halves):
        recon, states = scatter_sum(ring, block_rows, *shares[h])
        turned_rows.append(turned(after(gathered[h], states[-1])))
        misfit = recon - half_of(goal_block, h).astype(f32)
        loss_part = loss_part + 0.5 * jnp.sum(misfit * misfit)
        payload = misfit.astype(bf16)
        if h == halves - 1:
            three = jnp.stack(split_three(loss_part))
            tail = jnp.broadcast_to(jnp.pad(three, (0, PAD - 3))[None, :], (block_rows, PAD))
            payload = jnp.concatenate([payload, tail], axis=1)
        errors.append(gather(ring, core, payload)[0])
    loss_sum = sum(
        jnp.sum(piece[::block_rows, width : width + 3].astype(f32)) for piece in errors[-1]
    )
    whole = loss_sum
    for _ in range(layers - 1):
        loss_sum = lax.ppermute(
            loss_sum, "layer", [(i, (i + 1) % layers) for i in range(layers)]
        )
        whole = whole + loss_sum
    loss = whole / (layers * tokens * width)

    coef = (penalty_weight * act_sum / row_norms)[:, None]
    enc_grad, bias_grad, dec_grad = backward(
        errors, acts, gates, turned_rows, decoder, row_norms[None, :], coef
    )
    return enc_grad[None], bias_grad, dec_grad[None], loss


def solution(mesh):
    return jax.shard_map(
        body,
        mesh=mesh,
        in_specs=(
            P("layer", "feat", None),
            P("layer", "feat", None),
            P("layer", None, "feat"),
            P("layer", "feat"),
            P("layer", "feat", None),
            P("layer", None, "feat"),
        ),
        out_specs=(P("layer", None, "feat"), P("layer", "feat"), P("layer", "feat", None), P()),
        check_vma=False,
    )
```

```python
import functools

import jax
import jax.numpy as jnp
import numpy as np
from jax import lax
from jax.experimental import pallas as pl
from jax.experimental.pallas import tpu as pltpu
from jax.sharding import PartitionSpec as P

TBLOCK = 128
FBLOCK = 128
PAD = 128

penalty_weight = 0.5
norm_epsilon = 1e-06
f32 = jnp.float32
bf16 = jnp.bfloat16


class Ring:
    def __init__(self, size):
        chips = size // 2
        self.hops = (chips - 1) // 2
        self.far = chips % 2 == 0
        order = list(range(0, chips, 2)) + list(range(1, chips, 2))[::-1]
        place = {chip: at for at, chip in enumerate(order)}
        self.step = []
        owners = []
        for device in range(size):
            chip, core = divmod(device, 2)
            at = place[chip]
            ahead = 1 if core == 0 else -1
            self.step.append((device, order[(at + ahead) % chips] * 2 + core))
            behind = [order[(at - ahead * k) % chips] for k in range(1, self.hops + 1)]
            front = [order[(at + ahead * k) % chips] for k in range(1, self.hops + 1)]
            last = [order[(at + self.hops + 1) % chips]] if self.far else []
            owners.append([2 * c + i for c in [chip] + behind + front + last for i in (0, 1)])
        self.owners = np.array(owners, np.int32)
        self.twin = [(device, device ^ 1) for device in range(size)]

    def along(self, block):
        return lax.ppermute(block, "feat", self.step)

    def across(self, block):
        return lax.ppermute(block, "feat", self.twin)


def after(values, signal):
    return lax.optimization_barrier((values, signal))[0]


def gather(ring, block):
    behind = []
    moving = block
    for _ in range(ring.hops):
        moving = ring.along(moving)
        behind.append(moving)
    parts = [block]
    if behind:
        stack = jnp.concatenate(behind, axis=0)
        parts += [stack, ring.across(stack)]
    if ring.far:
        parts.append(ring.along(moving))
    return parts, behind


def scatter_sum(ring, first_core, rows, own, sent, front, last):
    from_twin = ring.across(sent)
    arrived = None
    states = []
    if ring.far:
        total = last + from_twin[rows * ring.hops :].astype(f32)
        half = rows // 2
        total = jnp.where(first_core, total[:half], total[half:])
        half_sum = ring.along(total.astype(bf16))
        states.append(half_sum)
        nothing = jnp.zeros_like(half_sum)
        arrived = jnp.concatenate(
            [jnp.where(first_core, half_sum, nothing), jnp.where(first_core, nothing, half_sum)], axis=0
        )
    for k in range(ring.hops, 0, -1):
        total = front[rows * (k - 1) : rows * k]
        total = total + from_twin[rows * (k - 1) : rows * k].astype(f32)
        if arrived is not None:
            total = total + arrived.astype(f32)
        arrived = ring.along(total.astype(bf16))
        states.append(arrived)
    total = own
    if arrived is not None:
        total = total + arrived.astype(f32)
    mine = total.astype(bf16)
    return mine, ring.across(mine), states


def chip_block(ring, first_core, own):
    other = ring.across(own)
    return jnp.concatenate(
        [jnp.where(first_core, own, other), jnp.where(first_core, other, own)], axis=0
    )


def in_vmem(x):
    return pltpu.with_memory_space_constraint(x, pltpu.VMEM)


VMEM_SPEC = pl.BlockSpec(memory_space=pltpu.VMEM)
ANY_SPEC = pl.BlockSpec(memory_space=pl.ANY)


def stacked(refs, columns):
    return jnp.concatenate([ref[:, columns] for ref in refs], axis=0)


def whole_pieces(parts):
    if all(p.shape[0] % 16 == 0 for p in parts):
        return parts
    return [jnp.concatenate(parts, axis=0)]


def forward_kernel(count, step, *refs):
    pieces = refs[:count]
    enc_ref, bias_ref, token_ref, mask_ref, dec_ref = refs[count : count + 5]
    act_ref, gate_ref, sum_ref = refs[count + 5 : count + 8]
    outs = refs[count + 8 :]
    width = dec_ref.shape[1]
    preact = jnp.zeros(gate_ref.shape, f32)
    for at in range(0, width, step):
        preact = preact + jnp.dot(
            stacked(pieces, slice(at, at + step)), enc_ref[at : at + step, :], preferred_element_type=f32
        )
    positive = jnp.maximum(preact + bias_ref[...], 0.0)
    token_block = token_ref[...]
    keep = jnp.zeros(gate_ref.shape, f32)
    for b in range(mask_ref.shape[0]):
        keep = jnp.where(token_block == b, mask_ref[b : b + 1, :], keep)
    act = (keep * positive * positive).astype(bf16)
    act_ref[...] = act
    gate_ref[...] = keep * 2.0 * positive
    sum_ref[...] = jnp.sum(act.astype(f32), axis=0, keepdims=True)
    for at in range(0, width, step):
        part = jnp.dot(act, dec_ref[:, at : at + step], preferred_element_type=f32)
        if len(outs) == 1:
            outs[0][:, at : at + step] = part
            continue
        own_ref, sent_ref, front_ref, last_ref = outs
        rows, hop = own_ref.shape[0], front_ref.shape[0]
        own_ref[:, at : at + step] = part[:rows]
        sent_ref[:hop, at : at + step] = part[rows : rows + hop].astype(bf16)
        sent_ref[hop:, at : at + step] = part[rows + 2 * hop :].astype(bf16)
        front_ref[:, at : at + step] = part[rows + hop : rows + 2 * hop]
        last_ref[:, at : at + step] = part[rows + 2 * hop :]


def forward(parts, encoder, bias, token_block, mask, decoder):
    pieces = whole_pieces(parts)
    total, features = token_block.shape[0], mask.shape[1]
    width = decoder.shape[1]
    shapes = [((total, features), bf16), ((total, features), f32), ((1, features), f32)]
    if len(pieces) == 4:
        rows, hop = parts[0].shape[0], parts[1].shape[0]
        shapes += [((rows, width), f32), ((hop + rows, width), bf16), ((hop, width), f32), ((rows, width), f32)]
    else:
        shapes += [((total, width), f32)]
    flops = 4 * total * features * width
    outs = pl.pallas_call(
        functools.partial(forward_kernel, len(pieces), min(512, width)),
        out_shape=[pltpu.VMEM(shape, dtype) for shape, dtype in shapes],
        in_specs=[VMEM_SPEC] * (len(pieces) + 5),
        out_specs=[VMEM_SPEC] * len(shapes),
        compiler_params=pltpu.CompilerParams(vmem_limit_bytes=12 << 20),
        cost_estimate=pl.CostEstimate(flops=flops, bytes_accessed=1 << 20, transcendentals=0),
    )(*[in_vmem(x) for x in (*pieces, encoder, bias, token_block, mask, decoder)])
    act, gate, act_sum = outs[:3]
    if len(outs) > 4:
        return act, gate, act_sum, outs[3:]
    full = outs[3]
    sizes = [p.shape[0] for p in parts]
    ends = np.cumsum([0] + sizes)
    cut = [full[ends[i] : ends[i + 1]] for i in range(len(sizes))]
    own = cut[0]
    hop = sizes[1] if len(sizes) > 2 else 0
    front = full[ends[2] : ends[3]] if hop else None
    last = cut[-1] if len(sizes) % 2 == 0 else full[:0]
    behind = full[ends[1] : ends[2]] if hop else full[:0]
    sent = jnp.concatenate([behind, last], axis=0).astype(bf16)
    return act, gate, act_sum, (own, sent, front, last)


def turn_kernel(*refs):
    pieces, out_ref = refs[:-1], refs[-1]
    step = 128 if out_ref.shape[0] % 128 == 0 else out_ref.shape[0]
    for at in range(0, out_ref.shape[0], step):
        out_ref[at : at + step, :] = stacked(pieces, slice(at, at + step)).T


def turned(parts):
    pieces = whole_pieces(parts)
    total = sum(p.shape[0] for p in pieces)
    width = pieces[0].shape[1]
    return pl.pallas_call(
        turn_kernel,
        out_shape=pltpu.VMEM((width, total), bf16),
        in_specs=[VMEM_SPEC] * len(pieces),
        out_specs=VMEM_SPEC,
        compiler_params=pltpu.CompilerParams(vmem_limit_bytes=12 << 20),
        cost_estimate=pl.CostEstimate(flops=0, bytes_accessed=4 << 20, transcendentals=0),
    )(*[in_vmem(x) for x in pieces])


def backward_kernel(counts, step, *refs):
    halves = len(counts)
    at = sum(counts)
    errors = refs[:at]
    acts, gates, rows = (refs[at + halves * i : at + halves * (i + 1)] for i in range(3))
    dec_ref, norm_ref, coef_ref = refs[at + 3 * halves : at + 3 * halves + 3]
    enc_out, bias_out, dec_out = refs[at + 3 * halves + 3 : at + 3 * halves + 6]
    enc_stage, dec_stage, enc_sems, dec_sems = refs[at + 3 * halves + 6 :]
    features, width = dec_ref.shape
    turned_act = jnp.concatenate([a[...] for a in acts], axis=0).T
    coef = coef_ref[...]
    copies = []
    for i, at in enumerate(range(0, width, step)):
        columns = slice(at, at + step)
        grad = jnp.dot(turned_act, stacked(errors, columns), preferred_element_type=f32)
        grad = grad + coef * dec_ref[:, columns].astype(f32)
        dec_stage[:, columns] = grad.astype(bf16)
        copy = pltpu.make_async_copy(dec_stage.at[:, columns], dec_out.at[:, columns], dec_sems.at[i])
        copy.start()
        copies.append(copy)
    total = turned_act.shape[1]
    act_grad = jnp.zeros((total, features), f32)
    for at in range(0, width, step):
        columns = slice(at, at + step)
        act_grad = act_grad + lax.dot_general(
            stacked(errors, columns), dec_ref[:, columns], (((1,), (1,)), ((), ())), preferred_element_type=f32
        )
    gate = jnp.concatenate([g[...] for g in gates], axis=0)
    pre_grad = ((act_grad + penalty_weight * norm_ref[...]) * gate).astype(bf16)
    bias_out[...] = jnp.sum(pre_grad.astype(f32), axis=0, keepdims=True)
    for i, at in enumerate(range(0, width, step)):
        here = slice(at, at + step)
        left = jnp.concatenate([r[here, :] for r in rows], axis=1)
        enc_stage[here, :] = jnp.dot(left, pre_grad, preferred_element_type=f32).astype(bf16)
        copy = pltpu.make_async_copy(enc_stage.at[here, :], enc_out.at[here, :], enc_sems.at[i])
        copy.start()
        copies.append(copy)
    for copy in copies:
        copy.wait()


def backward(errors, acts, gates, rows, decoder, norms, coef):
    errors = [whole_pieces(e) for e in errors]
    features, width = decoder.shape
    step = min(512, width)
    operands = [x for e in errors for x in e] + acts + gates + rows + [decoder, norms, coef]
    total = sum(a.shape[0] for a in acts)
    return pl.pallas_call(
        functools.partial(backward_kernel, tuple(len(e) for e in errors), step),
        out_shape=[
            jax.ShapeDtypeStruct((width, features), bf16),
            jax.ShapeDtypeStruct((1, features), f32),
            jax.ShapeDtypeStruct((features, width), bf16),
        ],
        in_specs=[VMEM_SPEC] * len(operands),
        out_specs=[ANY_SPEC, VMEM_SPEC, ANY_SPEC],
        scratch_shapes=[
            pltpu.VMEM((width, features), bf16),
            pltpu.VMEM((features, width), bf16),
            pltpu.SemaphoreType.DMA((width // step,)),
            pltpu.SemaphoreType.DMA((width // step,)),
        ],
        compiler_params=pltpu.CompilerParams(vmem_limit_bytes=24 << 20),
        cost_estimate=pl.CostEstimate(flops=6 * total * features * width, bytes_accessed=8 << 20, transcendentals=0),
    )(*[in_vmem(x) for x in operands])


def norm_kernel(halves, step, *refs):
    sums, dec_ref = refs[:halves], refs[halves]
    norm_ref, coef_ref, penalty_ref = refs[halves + 1 :]
    features, width = dec_ref.shape
    partial = jnp.zeros((features, 128), f32)
    for at in range(0, width, 128):
        part = dec_ref[:, at : at + 128].astype(f32)
        partial = partial + part * part
    squares = jnp.sum(partial.T, axis=0, keepdims=True)
    norm = jnp.sqrt(squares + norm_epsilon)
    act_sum = functools.reduce(jnp.add, [r[...] for r in sums])
    norm_ref[...] = norm
    penalty_ref[...] = penalty_weight * act_sum * norm
    coef = penalty_weight * act_sum / norm
    coef_ref[...] = jnp.broadcast_to(coef, (8, features)).T[:, :1]


def norms(sums, decoder):
    features = decoder.shape[0]
    return pl.pallas_call(
        functools.partial(norm_kernel, len(sums), 128),
        out_shape=[pltpu.VMEM(shape, f32) for shape in ((1, features), (features, 1), (1, features))],
        in_specs=[VMEM_SPEC] * (len(sums) + 1),
        out_specs=[VMEM_SPEC] * 3,
        compiler_params=pltpu.CompilerParams(vmem_limit_bytes=8 << 20),
        cost_estimate=pl.CostEstimate(flops=0, bytes_accessed=4 << 20, transcendentals=0),
    )(*[in_vmem(x) for x in (*sums, decoder)])


def misfit_kernel(carries_loss, *refs):
    mine_ref, other_ref, goal_ref = refs[:3]
    rest, out_ref = refs[3:-2], refs[-2]
    width = mine_ref.shape[1]
    misfit = mine_ref[...].astype(f32) + other_ref[...].astype(f32) - goal_ref[...].astype(f32)
    loss = 0.5 * jnp.sum(misfit * misfit, keepdims=True)
    for ref in rest:
        loss = loss + jnp.sum(ref[...], keepdims=True)
    refs[-1][...] = loss
    out_ref[:, :width] = misfit.astype(bf16)
    if carries_loss:
        high = loss.astype(bf16).astype(f32)
        middle = (loss - high).astype(bf16).astype(f32)
        low = loss - high - middle
        lane = lax.broadcasted_iota(jnp.int32, (out_ref.shape[0], PAD), 1)
        tail = jnp.where(lane == 0, high, jnp.where(lane == 1, middle, jnp.where(lane == 2, low, 0.0)))
        out_ref[:, width:] = tail.astype(bf16)


def misfits(mine, other, goal, rest, carries_loss):
    rows, width = mine.shape
    operands = (mine, other, goal, *rest)
    return pl.pallas_call(
        functools.partial(misfit_kernel, carries_loss),
        out_shape=[
            pltpu.VMEM((rows, width + PAD if carries_loss else width), bf16),
            pltpu.VMEM((1, 1), f32),
        ],
        in_specs=[VMEM_SPEC] * len(operands),
        out_specs=[VMEM_SPEC] * 2,
        compiler_params=pltpu.CompilerParams(vmem_limit_bytes=8 << 20),
        cost_estimate=pl.CostEstimate(flops=0, bytes_accessed=1 << 20, transcendentals=0),
    )(*[in_vmem(x) for x in operands])


def loss_kernel(scale, *refs):
    pieces, out_ref = refs[:-1], refs[-1]
    total = jnp.zeros((1, 1), f32)
    for ref in pieces:
        tail = ref[:, ref.shape[1] - PAD :].astype(f32)
        total = total + jnp.sum(tail, keepdims=True)
    out_ref[...] = jnp.broadcast_to(total * scale, out_ref.shape)


def group_loss(parts, block_rows):
    pieces = whole_pieces(parts)
    return pl.pallas_call(
        functools.partial(loss_kernel, 1.0 / block_rows),
        out_shape=pltpu.VMEM((8, PAD), f32),
        in_specs=[VMEM_SPEC] * len(pieces),
        out_specs=VMEM_SPEC,
        compiler_params=pltpu.CompilerParams(vmem_limit_bytes=8 << 20),
        cost_estimate=pl.CostEstimate(flops=0, bytes_accessed=1 << 16, transcendentals=0),
    )(*[in_vmem(x) for x in pieces])


def body(residual, targets, w_enc, b_enc, w_dec, block_mask):
    row_count = residual.shape[1]
    width = residual.shape[2]
    layers = lax.axis_size("layer")
    feats = lax.axis_size("feat")
    tokens = row_count * feats
    ring = Ring(feats)
    device = lax.axis_index("feat")
    first_core = device % 2 == 0
    halves = 2 if row_count % 16 == 0 else 1
    rows = row_count // halves
    block_rows = 2 * rows

    def half_of(block, h):
        return jnp.concatenate(
            [block[c * row_count + h * rows : c * row_count + (h + 1) * rows] for c in (0, 1)], axis=0
        )

    tokens_of = ring.owners[:, None, :, None] * row_count + np.arange(halves)[:, None, None] * rows + np.arange(rows)
    table = (tokens_of // TBLOCK).reshape(feats, halves, -1, 1).astype(np.int32)
    token_blocks = jnp.asarray(table)[device]

    own_block = chip_block(ring, first_core, residual[0])
    gathered, steps = [], []
    for h in range(halves):
        parts, behind = gather(ring, half_of(own_block, h))
        gathered.append(parts)
        steps.append(behind)
    targets, b_enc, block_mask = after((targets, b_enc, block_mask), steps[0][0])
    goal = lax.ppermute(targets[0], "layer", [(i, (i - 1) % layers) for i in range(layers)])
    goal_block = chip_block(ring, first_core, goal)
    mask = jnp.repeat(block_mask[0].astype(f32), FBLOCK, axis=1)
    encoder = w_enc[0]
    decoder = w_dec[0]

    acts, gates, shares, sums = [], [], [], []
    for h in range(halves):
        act, gate, act_sum, share = forward(gathered[h], encoder, b_enc, token_blocks[h], mask, decoder)
        acts.append(act)
        gates.append(gate)
        shares.append(share)
        sums.append(act_sum)
    summed = [scatter_sum(ring, first_core, block_rows, *share) for share in shares]
    norm, coef, penalty = norms(sums, after(decoder, summed[0][2][0]))
    rest = [penalty, ring.across(penalty)]
    errors, turned_rows = [], []
    for h in range(halves):
        mine, other, states = summed[h]
        turned_rows.append(turned(after(gathered[h], states[-1])))
        last = h == halves - 1
        payload, half_loss = misfits(mine, other, half_of(goal_block, h), rest if last else [], last)
        rest.append(half_loss)
        errors.append(gather(ring, payload)[0])
    sent_loss = loss_row = group_loss(errors[-1], block_rows)
    for _ in range(layers - 1):
        sent_loss = lax.ppermute(sent_loss, "layer", [(i, (i + 1) % layers) for i in range(layers)])
        loss_row = loss_row + sent_loss
    enc_grad, bias_grad, dec_grad = backward(errors, acts, gates, turned_rows, decoder, norm, coef)
    loss = after(loss_row, bias_grad)[0, 0] / (layers * tokens * width)
    return enc_grad[None], bias_grad, dec_grad[None], loss


def solution(mesh):
    return jax.shard_map(
        body,
        mesh=mesh,
        in_specs=(
            P("layer", "feat", None),
            P("layer", "feat", None),
            P("layer", None, "feat"),
            P("layer", "feat"),
            P("layer", "feat", None),
            P("layer", None, "feat"),
        ),
        out_specs=(P("layer", None, "feat"), P("layer", "feat"), P("layer", "feat", None), P()),
        check_vma=False,
    )
```

```python
import functools

import jax
import jax.numpy as jnp
import numpy as np
from jax import lax
from jax.experimental import pallas as pl
from jax.experimental.pallas import tpu as pltpu
from jax.sharding import PartitionSpec as P

TBLOCK = 128
FBLOCK = 128
PAD = 128

penalty_weight = 0.5
norm_epsilon = 1e-06
f32 = jnp.float32
bf16 = jnp.bfloat16


class Ring:
    def __init__(self, size):
        chips = size // 2
        self.hops = (chips - 1) // 2
        self.far = chips % 2 == 0
        order = list(range(0, chips, 2)) + list(range(1, chips, 2))[::-1]
        place = {chip: at for at, chip in enumerate(order)}
        self.step = []
        owners = []
        for device in range(size):
            chip, core = divmod(device, 2)
            at = place[chip]
            ahead = 1 if core == 0 else -1
            self.step.append((device, order[(at + ahead) % chips] * 2 + core))
            behind = [order[(at - ahead * k) % chips] for k in range(1, self.hops + 1)]
            front = [order[(at + ahead * k) % chips] for k in range(1, self.hops + 1)]
            last = [order[(at + self.hops + 1) % chips]] if self.far else []
            owners.append([2 * c + i for c in [chip] + behind + front + last for i in (0, 1)])
        self.owners = np.array(owners, np.int32)
        self.twin = [(device, device ^ 1) for device in range(size)]

    def along(self, block):
        return lax.ppermute(block, "feat", self.step)

    def across(self, block):
        return lax.ppermute(block, "feat", self.twin)


def after(value, *signals):
    return lax.optimization_barrier((value, *signals))[0]


class Turns:
    def __init__(self, halves, pins):
        self.ended = [[] for _ in range(halves)]
        self.pins = pins

    def enter(self, half, block):
        hop = len(self.ended[half])
        signals = [ends[hop - 2] for ends in self.ended if ends is not self.ended[half] and hop >= 2]
        if half == 0 and hop + 1 in self.pins:
            signals += self.pins[hop + 1](self.ended)
        return after(block, *signals)

    def leave(self, half, block):
        self.ended[half].append(block)


def gather(ring, blocks, pins, joint):
    halves = len(blocks)
    turns = Turns(halves, pins)
    moving = list(blocks)
    front = [[] for _ in blocks]
    for k in range(ring.hops + ring.far):
        for h in range(halves):
            block = after(moving[h], front[h][k - 2]) if k >= 2 else moving[h]
            moving[h] = ring.along(turns.enter(h, block))
            turns.leave(h, moving[h])
            if k < ring.hops:
                front[h].append(ring.across(moving[h]))
    parts = [[blocks[h]] + turns.ended[h][: ring.hops] + front[h] + turns.ended[h][ring.hops :] for h in range(halves)]
    if joint:
        last = ring.hops + ring.far + 1
        parts = after(parts, *(pins[last](turns.ended) if last in pins else []))
    return parts


def scatter_sums(ring, first_core, rows, shares, pins):
    halves = len(shares)
    turns = Turns(halves, pins)
    from_twin = [ring.across(sent) for _, sent, _, _ in shares]
    arrived = [None] * halves
    for k in range(ring.hops + ring.far, 0, -1):
        for h in range(halves):
            _, _, front, last = shares[h]
            if k > ring.hops:
                total = last + from_twin[h][rows * ring.hops :].astype(f32)
                half = rows // 2
                total = jnp.where(first_core, total[:half], total[half:])
            else:
                total = front[rows * (k - 1) : rows * k]
                total = total + from_twin[h][rows * (k - 1) : rows * k].astype(f32)
                if arrived[h] is not None:
                    total = total + arrived[h].astype(f32)
            came = ring.along(turns.enter(h, total.astype(bf16)))
            turns.leave(h, came)
            if k > ring.hops:
                nothing = jnp.zeros_like(came)
                came = jnp.concatenate(
                    [jnp.where(first_core, came, nothing), jnp.where(first_core, nothing, came)], axis=0
                )
            arrived[h] = came
    results = []
    for h in range(halves):
        total = shares[h][0]
        if arrived[h] is not None:
            total = total + arrived[h].astype(f32)
        mine = total.astype(bf16)
        results.append((mine, ring.across(mine)))
    return results


def pair_kernel(halves, own_ref, other_ref, *outs):
    first = lax.axis_index("feat") % 2 == 0
    own, other = own_ref[...].astype(f32), other_ref[...].astype(f32)
    low = jnp.where(first, own, other)
    high = jnp.where(first, other, own)
    rows = own.shape[0] // halves
    for h in range(halves):
        here = slice(h * rows, (h + 1) * rows)
        outs[h][...] = jnp.concatenate([low[here], high[here]], axis=0).astype(bf16)


def chip_blocks(own, other, halves):
    rows, width = own.shape[0] // halves, own.shape[1]
    return pl.pallas_call(
        functools.partial(pair_kernel, halves),
        out_shape=[pltpu.VMEM((2 * rows, width), own.dtype)] * halves,
        in_specs=[VMEM_SPEC] * 2,
        out_specs=[VMEM_SPEC] * halves,
        compiler_params=pltpu.CompilerParams(vmem_limit_bytes=8 << 20),
        cost_estimate=SHORT,
    )(in_vmem(own), in_vmem(other))


def in_vmem(x):
    return pltpu.with_memory_space_constraint(x, pltpu.VMEM)


def in_hbm(x):
    return pltpu.with_memory_space_constraint(x, pltpu.HBM)


VMEM_SPEC = pl.BlockSpec(memory_space=pltpu.VMEM)
ANY_SPEC = pl.BlockSpec(memory_space=pl.ANY)
HBM_SPEC = pl.BlockSpec(memory_space=pltpu.HBM)
SHORT = pl.CostEstimate(flops=0, bytes_accessed=0, transcendentals=0)
SMEM_SPEC = pl.BlockSpec(memory_space=pltpu.SMEM)


def stacked(refs, columns):
    return jnp.concatenate([ref[:, columns] for ref in refs], axis=0)


def whole_pieces(parts):
    if all(p.shape[0] % 16 == 0 for p in parts):
        return parts
    return [jnp.concatenate(parts, axis=0)]


def forward_kernel(count, step, *refs):
    pieces = refs[:count]
    enc_ref, bias_ref, keep_ref, dec_ref = refs[count : count + 4]
    act_ref, gate_ref, sum_ref = refs[count + 4 : count + 7]
    outs = refs[count + 7 :]
    width = dec_ref.shape[1]
    preact = jnp.zeros(gate_ref.shape, f32)
    for at in range(0, width, step):
        preact = preact + jnp.dot(
            stacked(pieces, slice(at, at + step)), enc_ref[at : at + step, :], preferred_element_type=f32
        )
    positive = jnp.maximum(preact + bias_ref[...], 0.0)
    keep = keep_ref[...]
    act = (keep * positive * positive).astype(bf16)
    act_ref[...] = act
    gate_ref[...] = keep * 2.0 * positive
    sum_ref[...] = jnp.sum(act.astype(f32), axis=0, keepdims=True)
    for at in range(0, width, step):
        part = jnp.dot(act, dec_ref[:, at : at + step], preferred_element_type=f32)
        if len(outs) == 1:
            outs[0][:, at : at + step] = part
            continue
        own_ref, sent_ref, front_ref, last_ref = outs
        rows, hop = own_ref.shape[0], front_ref.shape[0]
        own_ref[:, at : at + step] = part[:rows]
        sent_ref[:hop, at : at + step] = part[rows : rows + hop].astype(bf16)
        sent_ref[hop:, at : at + step] = part[rows + 2 * hop :].astype(bf16)
        front_ref[:, at : at + step] = part[rows + hop : rows + 2 * hop]
        last_ref[:, at : at + step] = part[rows + 2 * hop :]


def forward(ring, parts, encoder, bias, keep, decoder):
    pieces = whole_pieces(parts)
    rows, features = parts[0].shape[0], encoder.shape[1]
    total = sum(p.shape[0] for p in parts)
    hop = rows * ring.hops
    width = decoder.shape[1]
    shapes = [((total, features), bf16), ((total, features), f32), ((1, features), f32)]
    apart = rows % 16 == 0 and ring.hops > 0 and ring.far
    if apart:
        shapes += [((rows, width), f32), ((hop + rows, width), bf16), ((hop, width), f32), ((rows, width), f32)]
    else:
        shapes += [((total, width), f32)]
    outs = pl.pallas_call(
        functools.partial(forward_kernel, len(pieces), min(512, width)),
        out_shape=[pltpu.VMEM(shape, dtype) for shape, dtype in shapes],
        in_specs=[VMEM_SPEC] * (len(pieces) + 4),
        out_specs=[VMEM_SPEC] * len(shapes),
        compiler_params=pltpu.CompilerParams(vmem_limit_bytes=12 << 20),
        cost_estimate=SHORT,
    )(*[in_vmem(x) for x in (*pieces, encoder, bias, keep, decoder)])
    act, gate, act_sum = outs[:3]
    if apart:
        return act, gate, act_sum, outs[3:]
    full = outs[3]
    own, behind, front, last = (
        full[:rows], full[rows : rows + hop], full[rows + hop : rows + 2 * hop], full[rows + 2 * hop :]
    )
    return act, gate, act_sum, (own, jnp.concatenate([behind, last], axis=0).astype(bf16), front, last)


def turn_kernel(*refs):
    pieces, out_ref = refs[:-1], refs[-1]
    step = 128 if out_ref.shape[0] % 128 == 0 else out_ref.shape[0]
    for at in range(0, out_ref.shape[0], step):
        out_ref[at : at + step, :] = stacked(pieces, slice(at, at + step)).T


def turned(parts):
    pieces = whole_pieces(parts)
    total = sum(p.shape[0] for p in pieces)
    width = pieces[0].shape[1]
    return pl.pallas_call(
        turn_kernel,
        out_shape=pltpu.VMEM((width, total), bf16),
        in_specs=[VMEM_SPEC] * len(pieces),
        out_specs=VMEM_SPEC,
        compiler_params=pltpu.CompilerParams(vmem_limit_bytes=12 << 20),
        cost_estimate=SHORT,
    )(*[in_vmem(x) for x in pieces])


def backward_kernel(counts, step, *refs):
    halves = len(counts)
    at = sum(counts)
    errors = refs[:at]
    acts, gates, rows = (refs[at + halves * i : at + halves * (i + 1)] for i in range(3))
    dec_ref, norm_ref, sum_ref = refs[at + 3 * halves : at + 3 * halves + 3]
    enc_out, bias_out, dec_out = refs[at + 3 * halves + 3 : at + 3 * halves + 6]
    enc_stage, dec_stage, enc_sems, dec_sems = refs[at + 3 * halves + 6 :]
    features, width = dec_ref.shape
    turned_act = jnp.concatenate([a[...] for a in acts], axis=0).T
    coef = penalty_weight * sum_ref[...] / norm_ref[...]
    coef = jnp.broadcast_to(coef, (8, features)).T[:, :1]
    copies = []
    for i, at in enumerate(range(0, width, step)):
        columns = slice(at, at + step)
        grad = jnp.dot(turned_act, stacked(errors, columns), preferred_element_type=f32)
        grad = grad + coef * dec_ref[:, columns].astype(f32)
        dec_stage[:, columns] = grad.astype(bf16)
        copy = pltpu.make_async_copy(dec_stage.at[:, columns], dec_out.at[:, columns], dec_sems.at[i])
        copy.start()
        copies.append(copy)
    total = turned_act.shape[1]
    act_grad = jnp.zeros((total, features), f32)
    for at in range(0, width, step):
        columns = slice(at, at + step)
        act_grad = act_grad + lax.dot_general(
            stacked(errors, columns), dec_ref[:, columns], (((1,), (1,)), ((), ())), preferred_element_type=f32
        )
    gate = jnp.concatenate([g[...] for g in gates], axis=0)
    pre_grad = ((act_grad + penalty_weight * norm_ref[...]) * gate).astype(bf16)
    bias_out[...] = jnp.sum(pre_grad.astype(f32), axis=0, keepdims=True)
    for i, at in enumerate(range(0, width, step)):
        here = slice(at, at + step)
        left = jnp.concatenate([r[here, :] for r in rows], axis=1)
        enc_stage[here, :] = jnp.dot(left, pre_grad, preferred_element_type=f32).astype(bf16)
        copy = pltpu.make_async_copy(enc_stage.at[here, :], enc_out.at[here, :], enc_sems.at[i])
        copy.start()
        copies.append(copy)
    for copy in copies:
        copy.wait()


def backward(errors, acts, gates, rows, decoder, norms, act_sum):
    errors = [whole_pieces(e) for e in errors]
    features, width = decoder.shape
    step = min(512, width)
    operands = [x for e in errors for x in e] + acts + gates + rows + [decoder, norms, act_sum]
    total = sum(a.shape[0] for a in acts)
    return pl.pallas_call(
        functools.partial(backward_kernel, tuple(len(e) for e in errors), step),
        out_shape=[
            jax.ShapeDtypeStruct((width, features), bf16),
            jax.ShapeDtypeStruct((1, features), f32),
            jax.ShapeDtypeStruct((features, width), bf16),
        ],
        in_specs=[VMEM_SPEC] * len(operands),
        out_specs=[ANY_SPEC, VMEM_SPEC, ANY_SPEC],
        scratch_shapes=[
            pltpu.VMEM((width, features), bf16),
            pltpu.VMEM((features, width), bf16),
            pltpu.SemaphoreType.DMA((width // step,)),
            pltpu.SemaphoreType.DMA((width // step,)),
        ],
        compiler_params=pltpu.CompilerParams(vmem_limit_bytes=24 << 20),
        cost_estimate=SHORT,
    )(*[in_vmem(x) for x in operands])


def start_kernel(table_ref, own_ref, row_ref, out_ref, sems):
    copies = [
        pltpu.make_async_copy(own_ref, out_ref, sems.at[0]),
        pltpu.make_async_copy(table_ref.at[lax.axis_index("feat")], row_ref, sems.at[1]),
    ]
    for copy in copies:
        copy.start()
    for copy in copies:
        copy.wait()


def start(table, own):
    return pl.pallas_call(
        start_kernel,
        out_shape=[pltpu.VMEM((1, table.shape[2]), f32), pltpu.VMEM(own.shape, own.dtype)],
        in_specs=[HBM_SPEC] * 2,
        out_specs=[VMEM_SPEC] * 2,
        scratch_shapes=[pltpu.SemaphoreType.DMA((2,))],
        compiler_params=pltpu.CompilerParams(vmem_limit_bytes=4 << 20),
        cost_estimate=SHORT,
    )(in_hbm(table), in_hbm(own))


def load_kernel(source_ref, signal_ref, out_ref, sems):
    pieces = sems.shape[0]
    rows = out_ref.shape[0] // pieces
    copies = []
    for i in range(pieces):
        here = slice(i * rows, (i + 1) * rows)
        copy = pltpu.make_async_copy(source_ref.at[here], out_ref.at[here], sems.at[i])
        copy.start()
        copies.append(copy)
    for copy in copies:
        copy.wait()


def loaded(array, signal):
    return pl.pallas_call(
        load_kernel,
        out_shape=pltpu.VMEM(array.shape, array.dtype),
        in_specs=[HBM_SPEC, VMEM_SPEC],
        out_specs=VMEM_SPEC,
        scratch_shapes=[pltpu.SemaphoreType.DMA((8,))],
        compiler_params=pltpu.CompilerParams(vmem_limit_bytes=4 << 20),
        cost_estimate=SHORT,
    )(in_hbm(array), in_vmem(signal))


def keep_kernel(mask_ref, token_ref, signal_ref, *outs):
    token_block = jnp.broadcast_to(token_ref[...], (8, token_ref.shape[1])).T[:, :1]
    for h, out_ref in enumerate(outs):
        total = out_ref.shape[0]
        here = token_block[h * total : (h + 1) * total]
        for j in range(mask_ref.shape[1]):
            column = jnp.zeros((total, FBLOCK), f32)
            for b in range(mask_ref.shape[0]):
                column = jnp.where(here == b, mask_ref[b, j].astype(f32), column)
            out_ref[:, j * FBLOCK : (j + 1) * FBLOCK] = column


def keeps(mask, token_block, signal, halves):
    total, features = token_block.shape[1] // halves, mask.shape[1] * FBLOCK
    return pl.pallas_call(
        keep_kernel,
        out_shape=[pltpu.VMEM((total, features), f32)] * halves,
        in_specs=[SMEM_SPEC, VMEM_SPEC, VMEM_SPEC],
        out_specs=[VMEM_SPEC] * halves,
        compiler_params=pltpu.CompilerParams(vmem_limit_bytes=4 << 20),
        cost_estimate=SHORT,
    )(mask, in_vmem(token_block), in_vmem(signal))


def norm_kernel(dec_ref, signal_ref, norm_ref):
    features, width = dec_ref.shape
    partial = jnp.zeros((features, 128), f32)
    for at in range(0, width, 128):
        part = dec_ref[:, at : at + 128].astype(f32)
        partial = partial + part * part
    norm_ref[...] = jnp.sqrt(jnp.sum(partial.T, axis=0, keepdims=True) + norm_epsilon)


def norms(decoder, signal):
    return pl.pallas_call(
        norm_kernel,
        out_shape=pltpu.VMEM((1, decoder.shape[0]), f32),
        in_specs=[VMEM_SPEC] * 2,
        out_specs=VMEM_SPEC,
        compiler_params=pltpu.CompilerParams(vmem_limit_bytes=4 << 20),
        cost_estimate=SHORT,
    )(in_vmem(decoder), in_vmem(signal))


def misfit_kernel(*refs):
    mine_ref, other_ref, goal_ref = refs[:3]
    rest, out_ref = refs[3:-1], refs[-1]
    width = mine_ref.shape[1]
    misfit = mine_ref[...].astype(f32) + other_ref[...].astype(f32) - goal_ref[...].astype(f32)
    loss = 0.5 * jnp.sum(misfit * misfit, keepdims=True)
    for ref in rest:
        loss = loss + jnp.sum(ref[...], keepdims=True)
    high = loss.astype(bf16).astype(f32)
    middle = (loss - high).astype(bf16).astype(f32)
    low = loss - high - middle
    lane = lax.broadcasted_iota(jnp.int32, (out_ref.shape[0], PAD), 1)
    tail = jnp.where(lane == 0, high, jnp.where(lane == 1, middle, jnp.where(lane == 2, low, 0.0)))
    out_ref[:, :width] = misfit.astype(bf16)
    out_ref[:, width:] = tail.astype(bf16)


def misfits(mine, other, goal, rest):
    rows, width = mine.shape
    operands = (mine, other, goal, *rest)
    return pl.pallas_call(
        misfit_kernel,
        out_shape=pltpu.VMEM((rows, width + PAD), bf16),
        in_specs=[VMEM_SPEC] * len(operands),
        out_specs=VMEM_SPEC,
        compiler_params=pltpu.CompilerParams(vmem_limit_bytes=8 << 20),
        cost_estimate=SHORT,
    )(*[in_vmem(x) for x in operands])


def loss_kernel(scale, *refs):
    pieces, out_ref = refs[:-1], refs[-1]
    total = jnp.zeros((1, 1), f32)
    for ref in pieces:
        tail = ref[:, ref.shape[1] - PAD :].astype(f32)
        total = total + jnp.sum(tail, keepdims=True)
    out_ref[...] = jnp.broadcast_to(total * scale, out_ref.shape)


def group_loss(pieces, block_rows):
    return pl.pallas_call(
        functools.partial(loss_kernel, 1.0 / block_rows),
        out_shape=pltpu.VMEM((8, PAD), f32),
        in_specs=[VMEM_SPEC] * len(pieces),
        out_specs=VMEM_SPEC,
        compiler_params=pltpu.CompilerParams(vmem_limit_bytes=8 << 20),
        cost_estimate=SHORT,
    )(*[in_vmem(x) for x in pieces])


def body(residual, targets, w_enc, b_enc, w_dec, block_mask):
    row_count = residual.shape[1]
    width = residual.shape[2]
    layers = lax.axis_size("layer")
    feats = lax.axis_size("feat")
    tokens = row_count * feats
    ring = Ring(feats)
    device = lax.axis_index("feat")
    first_core = device % 2 == 0
    halves = 2 if row_count % 16 == 0 else 1
    rows = row_count // halves
    block_rows = 2 * rows

    tokens_of = ring.owners[:, None, :, None] * row_count + np.arange(halves)[:, None, None] * rows + np.arange(rows)
    table = jnp.asarray((tokens_of // TBLOCK).reshape(feats, 1, -1).astype(np.float32))

    own = residual[0]
    other = ring.across(own)
    token_block, own = start(table, own)
    other, first_core = lax.optimization_barrier((other, first_core))
    goal = after(targets[0], own)
    goal = lax.ppermute(goal, "layer", [(i, (i - 1) % layers) for i in range(layers)])
    held = {}

    def keep_in(ended):
        held["keep"] = keeps(block_mask[0], token_block, own_blocks[0], halves)
        return [goal, *held["keep"]]

    def encoder_in(ended):
        held["encoder"] = loaded(w_enc[0], ended[-1][0])
        return [held["encoder"]]

    def decoder_in(ended):
        held["decoder"] = loaded(w_dec[0], ended[-1][1])
        return [held["decoder"]]

    own_blocks = chip_blocks(own, other, halves)
    pins = {2: keep_in, 3: encoder_in, 4: decoder_in}
    gathered = gather(ring, own_blocks, pins, True)
    encoder, decoder = held["encoder"], held["decoder"]

    acts, gates, shares, sums = [], [], [], []
    for h in range(halves):
        act, gate, act_sum, share = forward(ring, gathered[h], encoder, b_enc, held["keep"][h], decoder)
        acts.append(act)
        gates.append(gate)
        shares.append(share)
        sums.append(act_sum)
    act_sum = sum(sums[1:], sums[0])

    def goals_in(ended):
        other_goal = ring.across(after(goal, ended[-1][0]))
        held["goal"] = chip_blocks(goal, other_goal, halves)
        return list(held["goal"])

    def norm_in(ended):
        held["norm"] = norms(decoder, ended[-1][0])
        return [held["norm"]]

    def rows_in(ended):
        penalty = penalty_weight * act_sum * held["norm"]
        held["rest"] = [penalty, ring.across(penalty)]
        held["turned"] = [turned(after(parts, ended[-1][1])) for parts in gathered]
        return held["turned"] + held["rest"]

    pins = {3: lambda ended: goals_in(ended) + norm_in(ended), 4: rows_in}
    summed = scatter_sums(ring, first_core, block_rows, shares, pins)
    norm = held["norm"]
    rest = held["rest"]
    payloads = [misfits(*summed[h], held["goal"][h], rest if h == 0 else []) for h in range(halves)]
    errors = gather(ring, payloads, {}, False)
    turned_rows = held["turned"]
    sent_loss = loss_row = group_loss([piece for parts in errors for piece in parts], block_rows)
    for _ in range(layers - 1):
        sent_loss = lax.ppermute(sent_loss, "layer", [(i, (i + 1) % layers) for i in range(layers)])
        loss_row = loss_row + sent_loss
    enc_grad, bias_grad, dec_grad = backward(errors, acts, gates, turned_rows, decoder, norm, act_sum)
    loss = after(loss_row, bias_grad)[0, 0] / (layers * tokens * width)
    return enc_grad[None], bias_grad, dec_grad[None], loss


def solution(mesh):
    return jax.shard_map(
        body,
        mesh=mesh,
        in_specs=(
            P("layer", "feat", None),
            P("layer", "feat", None),
            P("layer", None, "feat"),
            P("layer", "feat"),
            P("layer", "feat", None),
            P("layer", None, "feat"),
        ),
        out_specs=(P("layer", None, "feat"), P("layer", "feat"), P("layer", "feat", None), P()),
        check_vma=False,
    )
```

```python
import functools

import jax
import jax.numpy as jnp
import numpy as np
from jax import lax
from jax.experimental import pallas as pl
from jax.experimental.pallas import tpu as pltpu
from jax.sharding import PartitionSpec as P

TBLOCK = 128
FBLOCK = 128
PAD = 128

penalty_weight = 0.5
norm_epsilon = 1e-06
f32 = jnp.float32
bf16 = jnp.bfloat16


class Ring:
    def __init__(self, size):
        chips = size // 2
        self.hops = (chips - 1) // 2
        self.far = chips % 2 == 0
        order = list(range(0, chips, 2)) + list(range(1, chips, 2))[::-1]
        place = {chip: at for at, chip in enumerate(order)}
        self.step = []
        owners = []
        for device in range(size):
            chip, core = divmod(device, 2)
            at = place[chip]
            ahead = 1 if core == 0 else -1
            self.step.append((device, order[(at + ahead) % chips] * 2 + core))
            behind = [order[(at - ahead * k) % chips] for k in range(1, self.hops + 1)]
            front = [order[(at + ahead * k) % chips] for k in range(1, self.hops + 1)]
            last = [order[(at + self.hops + 1) % chips]] if self.far else []
            owners.append([[2 * c + i for c in [chip] + behind + front + last] for i in (core, 1 - core)])
        self.owners = np.array(owners, np.int32)
        self.twin = [(device, device ^ 1) for device in range(size)]

    def along(self, block):
        return lax.ppermute(block, "feat", self.step)

    def across(self, block):
        return lax.ppermute(block, "feat", self.twin)


def after(value, *signals):
    return lax.optimization_barrier((value, *signals))[0]


class Turns:
    def __init__(self, pins, leading):
        self.ended = [[], []]
        self.pins = pins
        self.leading = leading

    def enter(self, chain, block):
        hop = len(self.ended[chain])
        signals = self.ended[1 - chain][hop - 2 : hop - 1] if hop >= 2 else []
        if chain == self.leading and hop + 1 in self.pins:
            signals = signals + self.pins[hop + 1](self.ended)
        return after(block, *signals)

    def leave(self, chain, block):
        self.ended[chain].append(block)


def gather(ring, mine, twins, pins, direct):
    turns = Turns(pins, 0)
    moving = [mine, twins]
    front = [[], []]
    for k in range(ring.hops + ring.far):
        for chain in (0, 1):
            if k == ring.hops and chain == 1 and not direct:
                continue
            block = after(moving[chain], front[chain][k - 2]) if k >= 2 else moving[chain]
            moving[chain] = ring.along(turns.enter(chain, block))
            turns.leave(chain, moving[chain])
            if k < ring.hops:
                front[chain].append(ring.across(moving[chain]))
    last = [[], []]
    if ring.far:
        last = [[moving[0]], [moving[1] if direct else ring.across(moving[0])]]
    parts = [
        [block] + turns.ended[chain][: ring.hops] + front[1 - chain] + last[chain]
        for chain, block in enumerate((mine, twins))
    ]
    if 0 in pins:
        parts = after(parts, *pins[0](turns.ended))
    return parts


def scatter_sums(ring, rows, shares, pins):
    turns = Turns(pins, 1)
    (own, sent, front, last), (own_twin, sent_twin, front_twin, _) = shares
    received = [ring.across(sent), ring.across(sent_twin)]
    arrived = [None, None]

    def send(chain, share, addend):
        total = share + addend.astype(f32)
        if arrived[chain] is not None:
            total = total + arrived[chain].astype(f32)
        arrived[chain] = ring.along(turns.enter(chain, total.astype(bf16)))
        turns.leave(chain, arrived[chain])

    def part(array, k):
        return array[rows * (k - 1) : rows * k]

    for k in range(ring.hops, -1, -1):
        if k > 0:
            send(0, part(front_twin, k), part(received[0], k))
        if k < ring.hops:
            send(1, part(front, k + 1), part(received[1], k + 1))
        elif ring.far:
            send(1, last, received[1][rows * ring.hops :])
    totals = []
    for share, came in ((own, arrived[1]), (own_twin, arrived[0])):
        totals.append((share if came is None else share + came.astype(f32)).astype(bf16))
    from_twin = [ring.across(total) for total in totals]
    return [(totals[0], from_twin[1]), (totals[1], from_twin[0])]


def in_vmem(x):
    return pltpu.with_memory_space_constraint(x, pltpu.VMEM)


def in_hbm(x):
    return pltpu.with_memory_space_constraint(x, pltpu.HBM)


VMEM_SPEC = pl.BlockSpec(memory_space=pltpu.VMEM)
ANY_SPEC = pl.BlockSpec(memory_space=pl.ANY)
HBM_SPEC = pl.BlockSpec(memory_space=pltpu.HBM)
SHORT = pl.CostEstimate(flops=0, bytes_accessed=0, transcendentals=0)
SMEM_SPEC = pl.BlockSpec(memory_space=pltpu.SMEM)


def stacked(refs, columns):
    return jnp.concatenate([ref[:, columns] for ref in refs], axis=0)


def whole_pieces(parts):
    if all(p.shape[0] % 16 == 0 for p in parts):
        return parts
    return [jnp.concatenate(parts, axis=0)]


def forward_kernel(count, step, *refs):
    pieces = refs[:count]
    enc_refs, dec_refs = refs[count : count + 2], refs[count + 2 : count + 4]
    bias_ref, keep_ref, act_ref, gate_ref, sum_ref = refs[count + 4 : count + 9]
    outs = refs[count + 9 :]
    width = dec_refs[0].shape[1]
    cut = width // 2
    preact = bias_ref[...]
    for i, enc_ref in enumerate(enc_refs):
        for at in range(0, cut, 512):
            preact = preact + jnp.dot(
                stacked(pieces, slice(i * cut + at, i * cut + at + 512)),
                enc_ref[at : at + 512, :],
                preferred_element_type=f32,
            )
    positive = jnp.maximum(preact, 0.0)
    keep = keep_ref[...]
    act = (keep * positive * positive).astype(bf16)
    act_ref[...] = act
    gate_ref[...] = keep * 2.0 * positive
    sum_ref[...] = jnp.sum(act.astype(f32), axis=0, keepdims=True)
    for at in range(0, width, step):
        columns = jnp.concatenate([ref[:, at : at + step] for ref in dec_refs], axis=0)
        part = jnp.dot(act, columns, preferred_element_type=f32)
        if len(outs) == 1:
            outs[0][:, at : at + step] = part
            continue
        own_ref, sent_ref, front_ref = outs[:3]
        rows, hop = own_ref.shape[0], front_ref.shape[0]
        own_ref[:, at : at + step] = part[:rows]
        sent_ref[:hop, at : at + step] = part[rows : rows + hop].astype(bf16)
        front_ref[:, at : at + step] = part[rows + hop : rows + 2 * hop]
        if len(outs) == 4:
            outs[3][:, at : at + step] = part[rows + 2 * hop :]
        else:
            sent_ref[hop:, at : at + step] = part[rows + 2 * hop :].astype(bf16)


def forward(ring, parts, encoder, bias, keep, decoder, keeps_last):
    pieces = whole_pieces(parts)
    rows, features = parts[0].shape[0], encoder[0].shape[1]
    total = sum(p.shape[0] for p in parts)
    hop = rows * ring.hops
    end = rows + 2 * hop
    width = decoder[0].shape[1]
    shapes = [((total, features), bf16), ((total, features), f32), ((1, features), f32)]
    apart = rows % 16 == 0 and ring.hops > 0 and ring.far
    if apart and keeps_last:
        shapes += [((rows, width), f32), ((hop, width), bf16), ((hop, width), f32), ((rows, width), f32)]
    elif apart:
        shapes += [((rows, width), f32), ((hop + rows, width), bf16), ((hop, width), f32)]
    else:
        shapes += [((total, width), f32)]
    outs = pl.pallas_call(
        functools.partial(forward_kernel, len(pieces), min(512, width)),
        out_shape=[pltpu.VMEM(shape, dtype) for shape, dtype in shapes],
        in_specs=[VMEM_SPEC] * (len(pieces) + 6),
        out_specs=[VMEM_SPEC] * len(shapes),
        compiler_params=pltpu.CompilerParams(vmem_limit_bytes=12 << 20),
        cost_estimate=SHORT,
    )(*[in_vmem(x) for x in (*pieces, *encoder, *decoder, bias, keep)])
    act, gate, act_sum = outs[:3]
    if apart:
        own, sent, front, *last = outs[3:]
        return act, gate, act_sum, (own, sent, front, last[0] if last else None)
    full = outs[3]
    sent = full[rows : rows + hop]
    if not keeps_last:
        sent = jnp.concatenate([sent, full[end:]], axis=0)
    return act, gate, act_sum, (full[:rows], sent.astype(bf16), full[rows + hop : end], full[end:])


def turn_kernel(*refs):
    pieces, out_ref = refs[:-1], refs[-1]
    step = 128 if out_ref.shape[0] % 128 == 0 else out_ref.shape[0]
    for at in range(0, out_ref.shape[0], step):
        out_ref[at : at + step, :] = stacked(pieces, slice(at, at + step)).T


def turned(parts):
    pieces = whole_pieces(parts)
    total = sum(p.shape[0] for p in pieces)
    width = pieces[0].shape[1]
    return pl.pallas_call(
        turn_kernel,
        out_shape=pltpu.VMEM((width, total), bf16),
        in_specs=[VMEM_SPEC] * len(pieces),
        out_specs=VMEM_SPEC,
        compiler_params=pltpu.CompilerParams(vmem_limit_bytes=12 << 20),
        cost_estimate=SHORT,
    )(*[in_vmem(x) for x in pieces])


def backward_kernel(counts, step, *refs):
    halves = len(counts)
    at = sum(counts)
    errors = refs[:at]
    acts, gates, rows = (refs[at + halves * i : at + halves * (i + 1)] for i in range(3))
    *dec_refs, norm_ref, sum_ref = refs[at + 3 * halves : at + 3 * halves + 4]
    enc_out, bias_out, dec_out = refs[at + 3 * halves + 4 : at + 3 * halves + 7]
    enc_stage, dec_stage, enc_sems, dec_sems = refs[at + 3 * halves + 7 :]
    features, width = dec_stage.shape
    turned_act = jnp.concatenate([a[...] for a in acts], axis=0).T
    coef = penalty_weight * sum_ref[...] / norm_ref[...]
    coef = jnp.broadcast_to(coef, (8, features)).T[:, :1]
    copies = []
    for i, at in enumerate(range(0, width, step)):
        columns = slice(at, at + step)
        grad = jnp.dot(turned_act, stacked(errors, columns), preferred_element_type=f32)
        grad = grad + coef * jnp.concatenate([ref[:, columns] for ref in dec_refs], axis=0).astype(f32)
        dec_stage[:, columns] = grad.astype(bf16)
        copy = pltpu.make_async_copy(dec_stage.at[:, columns], dec_out.at[:, columns], dec_sems.at[i])
        copy.start()
        copies.append(copy)
    total = turned_act.shape[1]
    act_grad = jnp.zeros((total, features), f32)
    for at in range(0, width, 512):
        columns = slice(at, at + 512)
        act_grad = act_grad + lax.dot_general(
            stacked(errors, columns), stacked(dec_refs, columns), (((1,), (1,)), ((), ())), preferred_element_type=f32
        )
    gate = jnp.concatenate([g[...] for g in gates], axis=0)
    pre_grad = ((act_grad + penalty_weight * norm_ref[...]) * gate).astype(bf16)
    bias_out[...] = jnp.sum(pre_grad.astype(f32), axis=0, keepdims=True)
    for i, at in enumerate(range(0, width, step)):
        here = slice(at, at + step)
        left = jnp.concatenate([r[here, :] for r in rows], axis=1)
        enc_stage[here, :] = jnp.dot(left, pre_grad, preferred_element_type=f32).astype(bf16)
        copy = pltpu.make_async_copy(enc_stage.at[here, :], enc_out.at[here, :], enc_sems.at[i])
        copy.start()
        copies.append(copy)
    for copy in copies:
        copy.wait()


def backward(errors, acts, gates, rows, decoder, norms, act_sum):
    errors = [whole_pieces(e) for e in errors]
    features, width = sum(d.shape[0] for d in decoder), decoder[0].shape[1]
    step = min(512, width)
    operands = [x for e in errors for x in e] + acts + gates + rows + [*decoder, norms, act_sum]
    total = sum(a.shape[0] for a in acts)
    return pl.pallas_call(
        functools.partial(backward_kernel, tuple(len(e) for e in errors), step),
        out_shape=[
            jax.ShapeDtypeStruct((width, features), bf16),
            jax.ShapeDtypeStruct((1, features), f32),
            jax.ShapeDtypeStruct((features, width), bf16),
        ],
        in_specs=[VMEM_SPEC] * len(operands),
        out_specs=[ANY_SPEC, VMEM_SPEC, ANY_SPEC],
        scratch_shapes=[
            pltpu.VMEM((width, features), bf16),
            pltpu.VMEM((features, width), bf16),
            pltpu.SemaphoreType.DMA((width // step,)),
            pltpu.SemaphoreType.DMA((width // step,)),
        ],
        compiler_params=pltpu.CompilerParams(vmem_limit_bytes=24 << 20),
        cost_estimate=SHORT,
    )(*[in_vmem(x) for x in operands])


def load_kernel(first, source_ref, signal_ref, out_ref, sems):
    pieces = sems.shape[0]
    rows = out_ref.shape[0] // pieces
    copies = []
    for i in range(pieces):
        copy = pltpu.make_async_copy(
            source_ref.at[first + i * rows : first + (i + 1) * rows], out_ref.at[i * rows : (i + 1) * rows], sems.at[i]
        )
        copy.start()
        copies.append(copy)
    for copy in copies:
        copy.wait()


def loaded(array, part, signal):
    rows = array.shape[0] // 2
    return pl.pallas_call(
        functools.partial(load_kernel, part * rows),
        out_shape=pltpu.VMEM((rows, array.shape[1]), array.dtype),
        in_specs=[HBM_SPEC, VMEM_SPEC],
        out_specs=VMEM_SPEC,
        scratch_shapes=[pltpu.SemaphoreType.DMA((4,))],
        compiler_params=pltpu.CompilerParams(vmem_limit_bytes=4 << 20),
        cost_estimate=SHORT,
    )(in_hbm(array), in_vmem(signal))


def prepare_kernel(mask_ref, table_ref, half_ref, source_ref, signal_ref, dec_ref, norm_ref, *rest):
    keep_refs, (row_ref, row_sem, sems) = rest[:-3], rest[-3:]
    row = pltpu.make_async_copy(table_ref.at[lax.axis_index("feat")], row_ref, row_sem)
    row.start()
    pieces = sems.shape[0]
    rows, width = dec_ref.shape[0] // pieces, dec_ref.shape[1]
    copies = []
    for i in range(pieces):
        here = slice(i * rows, (i + 1) * rows)
        there = slice(dec_ref.shape[0] + i * rows, dec_ref.shape[0] + (i + 1) * rows)
        copy = pltpu.make_async_copy(source_ref.at[there], dec_ref.at[here], sems.at[i])
        copy.start()
        copies.append(copy)
    row.wait()
    token_block = jnp.broadcast_to(row_ref[...], (8, row_ref.shape[1])).T[:, :1]
    for i, out_ref in enumerate(keep_refs):
        total = out_ref.shape[0]
        here = token_block[i * total : (i + 1) * total]
        for j in range(mask_ref.shape[1]):
            column = jnp.zeros((total, FBLOCK), f32)
            for b in range(mask_ref.shape[0]):
                column = jnp.where(here == b, mask_ref[b, j].astype(f32), column)
            out_ref[:, j * FBLOCK : (j + 1) * FBLOCK] = column
    for half, ref in enumerate((half_ref, dec_ref)):
        for i in range(pieces):
            if half:
                copies[i].wait()
            here = slice(i * rows, (i + 1) * rows)
            partial = jnp.zeros((rows, 128), f32)
            for at in range(0, width, 128):
                part = ref[here, at : at + 128].astype(f32)
                partial = partial + part * part
            there = slice(half * dec_ref.shape[0] + i * rows, half * dec_ref.shape[0] + (i + 1) * rows)
            norm_ref[:, there] = jnp.sqrt(jnp.sum(partial.T, axis=0, keepdims=True) + norm_epsilon)


def prepared(mask, table, half, decoder, signal):
    features = decoder.shape[0]
    total = table.shape[2] // 2
    dec, norm, *keep = pl.pallas_call(
        prepare_kernel,
        out_shape=[
            pltpu.VMEM(half.shape, half.dtype),
            pltpu.VMEM((1, features), f32),
            pltpu.VMEM((total, features), f32),
            pltpu.VMEM((total, features), f32),
        ],
        in_specs=[SMEM_SPEC, HBM_SPEC, VMEM_SPEC, HBM_SPEC, VMEM_SPEC],
        out_specs=[VMEM_SPEC] * 4,
        scratch_shapes=[
            pltpu.VMEM((1, table.shape[2]), f32),
            pltpu.SemaphoreType.DMA,
            pltpu.SemaphoreType.DMA((max(1, half.shape[0] // 128),)),
        ],
        compiler_params=pltpu.CompilerParams(vmem_limit_bytes=4 << 20),
        cost_estimate=SHORT,
    )(mask, in_hbm(table), in_vmem(half), in_hbm(decoder), in_vmem(signal))
    return dec, norm, keep


def misfit_kernel(*refs):
    mine_ref, other_ref, goal_ref = refs[:3]
    rest, out_ref = refs[3:-1], refs[-1]
    width = mine_ref.shape[1]
    misfit = mine_ref[...].astype(f32) + other_ref[...].astype(f32) - goal_ref[...].astype(f32)
    loss = 0.5 * jnp.sum(misfit * misfit, keepdims=True)
    for ref in rest:
        loss = loss + jnp.sum(ref[...], keepdims=True)
    high = loss.astype(bf16).astype(f32)
    middle = (loss - high).astype(bf16).astype(f32)
    low = loss - high - middle
    lane = lax.broadcasted_iota(jnp.int32, (out_ref.shape[0], PAD), 1)
    tail = jnp.where(lane == 0, high, jnp.where(lane == 1, middle, jnp.where(lane == 2, low, 0.0)))
    out_ref[:, :width] = misfit.astype(bf16)
    out_ref[:, width:] = tail.astype(bf16)


def misfits(mine, other, goal, rest):
    rows, width = mine.shape
    operands = (mine, other, goal, *rest)
    return pl.pallas_call(
        misfit_kernel,
        out_shape=pltpu.VMEM((rows, width + PAD), bf16),
        in_specs=[VMEM_SPEC] * len(operands),
        out_specs=VMEM_SPEC,
        compiler_params=pltpu.CompilerParams(vmem_limit_bytes=8 << 20),
        cost_estimate=SHORT,
    )(*[in_vmem(x) for x in operands])


def loss_kernel(scale, *refs):
    pieces, out_ref = refs[:-1], refs[-1]
    total = jnp.zeros((1, 1), f32)
    for ref in pieces:
        tail = ref[:, ref.shape[1] - PAD :].astype(f32)
        total = total + jnp.sum(tail, keepdims=True)
    out_ref[...] = jnp.broadcast_to(total * scale, out_ref.shape)


def group_loss(pieces, block_rows):
    return pl.pallas_call(
        functools.partial(loss_kernel, 1.0 / block_rows),
        out_shape=pltpu.VMEM((8, PAD), f32),
        in_specs=[VMEM_SPEC] * len(pieces),
        out_specs=VMEM_SPEC,
        compiler_params=pltpu.CompilerParams(vmem_limit_bytes=8 << 20),
        cost_estimate=SHORT,
    )(*[in_vmem(x) for x in pieces])


def body(residual, targets, w_enc, b_enc, w_dec, block_mask):
    rows = residual.shape[1]
    width = residual.shape[2]
    layers = lax.axis_size("layer")
    feats = lax.axis_size("feat")
    tokens = rows * feats
    ring = Ring(feats)

    tokens_of = ring.owners[..., None] * rows + np.arange(rows)
    table = jnp.asarray((tokens_of // TBLOCK).reshape(feats, 1, -1).astype(np.float32))

    own = residual[0]
    twins = ring.across(own)
    held = {}

    def load_in(name, array, part, hop):
        def pin(ended):
            signal = ended[0][hop - 1] if hop else twins
            held[name, part] = loaded(array, part, signal)
            return [held[name, part]]

        return pin

    def rest_in(ended):
        held["decoder", 1], held["norm"], held["keep"] = prepared(
            block_mask[0], table, held["decoder", 0], w_dec[0], ended[1][ring.hops - 1]
        )
        return [held["decoder", 1], held["norm"], *held["keep"]]

    pins = {
        2: load_in("encoder", w_enc[0], 0, 0),
        3: load_in("encoder", w_enc[0], 1, 1),
        4: load_in("decoder", w_dec[0], 0, 2),
        0: rest_in,
    }
    gathered = gather(ring, own, twins, pins, True)
    encoder = [held["encoder", i] for i in (0, 1)]
    decoder = [held["decoder", i] for i in (0, 1)]

    acts, gates, sums, shares = zip(
        *[forward(ring, gathered[i], encoder, b_enc, held["keep"][i], decoder, i == 0) for i in (0, 1)]
    )
    act_sum = sums[0] + sums[1]

    def goals_in(ended):
        goal = after(targets[0], ended[0][0])
        goal = lax.ppermute(goal, "layer", [(i, (i - 1) % layers) for i in range(layers)])
        held["goal"] = [goal, ring.across(goal)]
        return list(held["goal"])

    def rest_in(ended):
        penalty = penalty_weight * act_sum * held["norm"]
        held["rest"] = [penalty, ring.across(penalty)]
        return held["rest"]

    pins = {4: lambda ended: goals_in(ended) + rest_in(ended)}
    summed = scatter_sums(ring, rows, shares, pins)
    payloads = [misfits(*summed[i], held["goal"][i], held["rest"][i : i + 1]) for i in (0, 1)]
    held["turned"] = []

    def rows_in(ended):
        chain = len(held["turned"])
        held["turned"].append(turned(after(gathered[chain], ended[1][chain])))
        return held["turned"][-1:]

    errors = gather(ring, *payloads, {3: rows_in, 4: rows_in}, False)
    sent_loss = loss_row = group_loss([piece for parts in errors for piece in parts], rows)
    for _ in range(layers - 1):
        sent_loss = lax.ppermute(sent_loss, "layer", [(i, (i + 1) % layers) for i in range(layers)])
        loss_row = loss_row + sent_loss
    enc_grad, bias_grad, dec_grad = backward(
        errors, list(acts), list(gates), held["turned"], decoder, held["norm"], act_sum
    )
    loss = after(loss_row, bias_grad)[0, 0] / (layers * tokens * width)
    return enc_grad[None], bias_grad, dec_grad[None], loss


def solution(mesh):
    return jax.shard_map(
        body,
        mesh=mesh,
        in_specs=(
            P("layer", "feat", None),
            P("layer", "feat", None),
            P("layer", None, "feat"),
            P("layer", "feat"),
            P("layer", "feat", None),
            P("layer", None, "feat"),
        ),
        out_specs=(P("layer", None, "feat"), P("layer", "feat"), P("layer", "feat", None), P()),
        check_vma=False,
    )
```

```python
import functools

import jax
import jax.numpy as jnp
import numpy as np
from jax import lax
from jax.experimental import pallas as pl
from jax.experimental.pallas import tpu as pltpu
from jax.sharding import PartitionSpec as P

TBLOCK = 128
FBLOCK = 128
PAD = 128

penalty_weight = 0.5
norm_epsilon = 1e-06
f32 = jnp.float32
bf16 = jnp.bfloat16


class Ring:
    def __init__(self, size):
        chips = size // 2
        self.hops = (chips - 1) // 2
        self.far = chips % 2 == 0
        order = list(range(0, chips, 2)) + list(range(1, chips, 2))[::-1]
        place = {chip: at for at, chip in enumerate(order)}
        self.step = []
        owners = []
        for device in range(size):
            chip, core = divmod(device, 2)
            at = place[chip]
            ahead = 1 if core == 0 else -1
            self.step.append((device, order[(at + ahead) % chips] * 2 + core))
            behind = [order[(at - ahead * k) % chips] for k in range(1, self.hops + 1)]
            front = [order[(at + ahead * k) % chips] for k in range(1, self.hops + 1)]
            last = [order[(at + self.hops + 1) % chips]] if self.far else []
            owners.append([[2 * c + i for c in [chip] + behind + front + last] for i in (core, 1 - core)])
        self.owners = np.array(owners, np.int32)
        self.twin = [(device, device ^ 1) for device in range(size)]

    def along(self, block):
        return lax.ppermute(block, "feat", self.step)

    def across(self, block):
        return lax.ppermute(block, "feat", self.twin)


def after(value, *signals):
    return lax.optimization_barrier((value, *signals))[0]


class Turns:
    def __init__(self, pins, leading):
        self.ended = [[], []]
        self.pins = pins
        self.leading = leading

    def enter(self, chain, block):
        hop = len(self.ended[chain])
        signals = self.ended[1 - chain][hop - 2 : hop - 1] if hop >= 2 else []
        if chain == self.leading and hop + 1 in self.pins:
            signals = signals + self.pins[hop + 1](self.ended)
        return after(block, *signals)

    def leave(self, chain, block):
        self.ended[chain].append(block)


def gather(ring, mine, twins, pins, direct):
    turns = Turns(pins, 0)
    moving = [mine, twins]
    front = [[], []]
    for k in range(ring.hops + ring.far):
        for chain in (0, 1):
            if k == ring.hops and chain == 1 and not direct:
                continue
            block = after(moving[chain], front[chain][k - 2]) if k >= 2 else moving[chain]
            moving[chain] = ring.along(turns.enter(chain, block))
            turns.leave(chain, moving[chain])
            if k < ring.hops:
                front[chain].append(ring.across(moving[chain]))
    last = [[], []]
    if ring.far:
        last = [[moving[0]], [moving[1] if direct else ring.across(moving[0])]]
    parts = [
        [block] + turns.ended[chain][: ring.hops] + front[1 - chain] + last[chain]
        for chain, block in enumerate((mine, twins))
    ]
    if 0 in pins:
        parts = after(parts, *pins[0](turns.ended))
    return parts


def scatter_sums(ring, rows, shares, pins):
    turns = Turns(pins, 1)
    (own, sent, front, last), (own_twin, sent_twin, front_twin, _) = shares
    received = [ring.across(sent), ring.across(sent_twin)]
    arrived = [None, None]

    def send(chain, share, addend):
        total = share + addend.astype(f32)
        if arrived[chain] is not None:
            total = total + arrived[chain].astype(f32)
        arrived[chain] = ring.along(turns.enter(chain, total.astype(bf16)))
        turns.leave(chain, arrived[chain])

    def part(array, k):
        return array[rows * (k - 1) : rows * k]

    for k in range(ring.hops, -1, -1):
        if k > 0:
            send(0, part(front_twin, k), part(received[0], k))
        if k < ring.hops:
            send(1, part(front, k + 1), part(received[1], k + 1))
        elif ring.far:
            send(1, last, received[1][rows * ring.hops :])
    totals = []
    for share, came in ((own, arrived[1]), (own_twin, arrived[0])):
        totals.append((share if came is None else share + came.astype(f32)).astype(bf16))
    from_twin = [ring.across(total) for total in totals]
    return [(totals[0], from_twin[1]), (totals[1], from_twin[0])]


def in_vmem(x):
    return pltpu.with_memory_space_constraint(x, pltpu.VMEM)


def in_hbm(x):
    return pltpu.with_memory_space_constraint(x, pltpu.HBM)


VMEM_SPEC = pl.BlockSpec(memory_space=pltpu.VMEM)
ANY_SPEC = pl.BlockSpec(memory_space=pl.ANY)
HBM_SPEC = pl.BlockSpec(memory_space=pltpu.HBM)
SHORT = pl.CostEstimate(flops=0, bytes_accessed=0, transcendentals=0)
SMEM_SPEC = pl.BlockSpec(memory_space=pltpu.SMEM)


def stacked(refs, columns):
    return jnp.concatenate([ref[:, columns] for ref in refs], axis=0)


def whole_pieces(parts):
    if all(p.shape[0] % 16 == 0 for p in parts):
        return parts
    return [jnp.concatenate(parts, axis=0)]


def forward_kernel(count, step, *refs):
    pieces = refs[:count]
    enc_refs, dec_refs = refs[count : count + 2], refs[count + 2 : count + 4]
    bias_ref, keep_ref, act_ref, gate_ref, sum_ref = refs[count + 4 : count + 9]
    outs = refs[count + 9 :]
    width = dec_refs[0].shape[1]
    cut = width // 2
    preact = bias_ref[...]
    for i, enc_ref in enumerate(enc_refs):
        for at in range(0, cut, 512):
            preact = preact + jnp.dot(
                stacked(pieces, slice(i * cut + at, i * cut + at + 512)),
                enc_ref[at : at + 512, :],
                preferred_element_type=f32,
            )
    positive = jnp.maximum(preact, 0.0)
    keep = keep_ref[...]
    act = (keep * positive * positive).astype(bf16)
    act_ref[...] = act
    gate_ref[...] = keep * 2.0 * positive
    sum_ref[...] = jnp.sum(act.astype(f32), axis=0, keepdims=True)
    for at in range(0, width, step):
        columns = jnp.concatenate([ref[:, at : at + step] for ref in dec_refs], axis=0)
        part = jnp.dot(act, columns, preferred_element_type=f32)
        if len(outs) == 1:
            outs[0][:, at : at + step] = part
            continue
        own_ref, sent_ref, front_ref = outs[:3]
        rows, hop = own_ref.shape[0], front_ref.shape[0]
        own_ref[:, at : at + step] = part[:rows]
        sent_ref[:hop, at : at + step] = part[rows : rows + hop].astype(bf16)
        front_ref[:, at : at + step] = part[rows + hop : rows + 2 * hop]
        if len(outs) == 4:
            outs[3][:, at : at + step] = part[rows + 2 * hop :]
        else:
            sent_ref[hop:, at : at + step] = part[rows + 2 * hop :].astype(bf16)


def forward(ring, parts, encoder, bias, keep, decoder, keeps_last):
    pieces = whole_pieces(parts)
    rows, features = parts[0].shape[0], encoder[0].shape[1]
    total = sum(p.shape[0] for p in parts)
    hop = rows * ring.hops
    end = rows + 2 * hop
    width = decoder[0].shape[1]
    shapes = [((total, features), bf16), ((total, features), f32), ((1, features), f32)]
    apart = rows % 16 == 0 and ring.hops > 0 and ring.far
    if apart and keeps_last:
        shapes += [((rows, width), f32), ((hop, width), bf16), ((hop, width), f32), ((rows, width), f32)]
    elif apart:
        shapes += [((rows, width), f32), ((hop + rows, width), bf16), ((hop, width), f32)]
    else:
        shapes += [((total, width), f32)]
    outs = pl.pallas_call(
        functools.partial(forward_kernel, len(pieces), min(512, width)),
        out_shape=[pltpu.VMEM(shape, dtype) for shape, dtype in shapes],
        in_specs=[VMEM_SPEC] * (len(pieces) + 6),
        out_specs=[VMEM_SPEC] * len(shapes),
        compiler_params=pltpu.CompilerParams(vmem_limit_bytes=12 << 20),
        cost_estimate=SHORT,
    )(*[in_vmem(x) for x in (*pieces, *encoder, *decoder, bias, keep)])
    act, gate, act_sum = outs[:3]
    if apart:
        own, sent, front, *last = outs[3:]
        return act, gate, act_sum, (own, sent, front, last[0] if last else None)
    full = outs[3]
    sent = full[rows : rows + hop]
    if not keeps_last:
        sent = jnp.concatenate([sent, full[end:]], axis=0)
    return act, gate, act_sum, (full[:rows], sent.astype(bf16), full[rows + hop : end], full[end:])


def turn_kernel(*refs):
    pieces, out_ref = refs[:-1], refs[-1]
    step = 128 if out_ref.shape[0] % 128 == 0 else out_ref.shape[0]
    for at in range(0, out_ref.shape[0], step):
        out_ref[at : at + step, :] = stacked(pieces, slice(at, at + step)).T


def turned(parts):
    pieces = whole_pieces(parts)
    total = sum(p.shape[0] for p in pieces)
    width = pieces[0].shape[1]
    return pl.pallas_call(
        turn_kernel,
        out_shape=pltpu.VMEM((width, total), bf16),
        in_specs=[VMEM_SPEC] * len(pieces),
        out_specs=VMEM_SPEC,
        compiler_params=pltpu.CompilerParams(vmem_limit_bytes=12 << 20),
        cost_estimate=SHORT,
    )(*[in_vmem(x) for x in pieces])


def backward_kernel(counts, step, *refs):
    halves = len(counts)
    at = sum(counts)
    errors = refs[:at]
    acts, gates, rows = (refs[at + halves * i : at + halves * (i + 1)] for i in range(3))
    *dec_refs, norm_ref, sum_ref = refs[at + 3 * halves : at + 3 * halves + 4]
    enc_out, bias_out, dec_out = refs[at + 3 * halves + 4 : at + 3 * halves + 7]
    enc_stage, dec_stage, enc_sems, dec_sems = refs[at + 3 * halves + 7 :]
    features, width = dec_stage.shape
    turned_act = jnp.concatenate([a[...] for a in acts], axis=0).T
    coef = penalty_weight * sum_ref[...] / norm_ref[...]
    coef = jnp.broadcast_to(coef, (8, features)).T[:, :1]
    copies = []
    for i, at in enumerate(range(0, width, step)):
        columns = slice(at, at + step)
        grad = jnp.dot(turned_act, stacked(errors, columns), preferred_element_type=f32)
        grad = grad + coef * jnp.concatenate([ref[:, columns] for ref in dec_refs], axis=0).astype(f32)
        dec_stage[:, columns] = grad.astype(bf16)
        copy = pltpu.make_async_copy(dec_stage.at[:, columns], dec_out.at[:, columns], dec_sems.at[i])
        copy.start()
        copies.append(copy)
    total = turned_act.shape[1]
    act_grad = jnp.zeros((total, features), f32)
    for at in range(0, width, 512):
        columns = slice(at, at + 512)
        act_grad = act_grad + lax.dot_general(
            stacked(errors, columns), stacked(dec_refs, columns), (((1,), (1,)), ((), ())), preferred_element_type=f32
        )
    gate = jnp.concatenate([g[...] for g in gates], axis=0)
    pre_grad = ((act_grad + penalty_weight * norm_ref[...]) * gate).astype(bf16)
    bias_out[...] = jnp.sum(pre_grad.astype(f32), axis=0, keepdims=True)
    for i, at in enumerate(range(0, width, step)):
        here = slice(at, at + step)
        left = jnp.concatenate([r[here, :] for r in rows], axis=1)
        enc_stage[here, :] = jnp.dot(left, pre_grad, preferred_element_type=f32).astype(bf16)
        copy = pltpu.make_async_copy(enc_stage.at[here, :], enc_out.at[here, :], enc_sems.at[i])
        copy.start()
        copies.append(copy)
    for copy in copies:
        copy.wait()


def backward(errors, acts, gates, rows, decoder, norms, act_sum):
    errors = [whole_pieces(e) for e in errors]
    features, width = sum(d.shape[0] for d in decoder), decoder[0].shape[1]
    step = min(512, width)
    operands = [x for e in errors for x in e] + acts + gates + rows + [*decoder, norms, act_sum]
    total = sum(a.shape[0] for a in acts)
    return pl.pallas_call(
        functools.partial(backward_kernel, tuple(len(e) for e in errors), step),
        out_shape=[
            jax.ShapeDtypeStruct((width, features), bf16),
            jax.ShapeDtypeStruct((1, features), f32),
            jax.ShapeDtypeStruct((features, width), bf16),
        ],
        in_specs=[VMEM_SPEC] * len(operands),
        out_specs=[ANY_SPEC, VMEM_SPEC, ANY_SPEC],
        scratch_shapes=[
            pltpu.VMEM((width, features), bf16),
            pltpu.VMEM((features, width), bf16),
            pltpu.SemaphoreType.DMA((width // step,)),
            pltpu.SemaphoreType.DMA((width // step,)),
        ],
        compiler_params=pltpu.CompilerParams(vmem_limit_bytes=24 << 20),
        cost_estimate=SHORT,
    )(*[in_vmem(x) for x in operands])


def load_kernel(first, source_ref, signal_ref, out_ref, sems):
    pieces = sems.shape[0]
    rows = out_ref.shape[0] // pieces
    copies = []
    for i in range(pieces):
        copy = pltpu.make_async_copy(
            source_ref.at[first + i * rows : first + (i + 1) * rows], out_ref.at[i * rows : (i + 1) * rows], sems.at[i]
        )
        copy.start()
        copies.append(copy)
    for copy in copies:
        copy.wait()


def loaded(array, part, signal):
    rows = array.shape[0] // 2
    return pl.pallas_call(
        functools.partial(load_kernel, part * rows),
        out_shape=pltpu.VMEM((rows, array.shape[1]), array.dtype),
        in_specs=[HBM_SPEC, VMEM_SPEC],
        out_specs=VMEM_SPEC,
        scratch_shapes=[pltpu.SemaphoreType.DMA((4,))],
        compiler_params=pltpu.CompilerParams(vmem_limit_bytes=4 << 20),
        cost_estimate=SHORT,
    )(in_hbm(array), in_vmem(signal))


def prepare_kernel(mask_ref, table_ref, half_ref, source_ref, signal_ref, dec_ref, norm_ref, *rest):
    keep_refs, (row_ref, row_sem, sems) = rest[:-3], rest[-3:]
    row = pltpu.make_async_copy(table_ref.at[lax.axis_index("feat")], row_ref, row_sem)
    row.start()
    pieces = sems.shape[0]
    rows, width = dec_ref.shape[0] // pieces, dec_ref.shape[1]
    copies = []
    for i in range(pieces):
        here = slice(i * rows, (i + 1) * rows)
        there = slice(dec_ref.shape[0] + i * rows, dec_ref.shape[0] + (i + 1) * rows)
        copy = pltpu.make_async_copy(source_ref.at[there], dec_ref.at[here], sems.at[i])
        copy.start()
        copies.append(copy)
    row.wait()
    token_block = jnp.broadcast_to(row_ref[...], (8, row_ref.shape[1])).T[:, :1]
    for i, out_ref in enumerate(keep_refs):
        total = out_ref.shape[0]
        here = token_block[i * total : (i + 1) * total]
        for j in range(mask_ref.shape[1]):
            column = jnp.zeros((total, FBLOCK), f32)
            for b in range(mask_ref.shape[0]):
                column = jnp.where(here == b, mask_ref[b, j].astype(f32), column)
            out_ref[:, j * FBLOCK : (j + 1) * FBLOCK] = column
    for half, ref in enumerate((half_ref, dec_ref)):
        for i in range(pieces):
            if half:
                copies[i].wait()
            here = slice(i * rows, (i + 1) * rows)
            partial = jnp.zeros((rows, 128), f32)
            for at in range(0, width, 128):
                part = ref[here, at : at + 128].astype(f32)
                partial = partial + part * part
            there = slice(half * dec_ref.shape[0] + i * rows, half * dec_ref.shape[0] + (i + 1) * rows)
            norm_ref[:, there] = jnp.sqrt(jnp.sum(partial.T, axis=0, keepdims=True) + norm_epsilon)


def prepared(mask, table, half, decoder, signal):
    features = decoder.shape[0]
    total = table.shape[2] // 2
    dec, norm, *keep = pl.pallas_call(
        prepare_kernel,
        out_shape=[
            pltpu.VMEM(half.shape, half.dtype),
            pltpu.VMEM((1, features), f32),
            pltpu.VMEM((total, features), f32),
            pltpu.VMEM((total, features), f32),
        ],
        in_specs=[SMEM_SPEC, HBM_SPEC, VMEM_SPEC, HBM_SPEC, VMEM_SPEC],
        out_specs=[VMEM_SPEC] * 4,
        scratch_shapes=[
            pltpu.VMEM((1, table.shape[2]), f32),
            pltpu.SemaphoreType.DMA,
            pltpu.SemaphoreType.DMA((max(1, half.shape[0] // 128),)),
        ],
        compiler_params=pltpu.CompilerParams(vmem_limit_bytes=4 << 20),
        cost_estimate=SHORT,
    )(mask, in_hbm(table), in_vmem(half), in_hbm(decoder), in_vmem(signal))
    return dec, norm, keep


def misfit_kernel(*refs):
    mine_ref, other_ref, goal_ref = refs[:3]
    rest, out_ref = refs[3:-1], refs[-1]
    width = mine_ref.shape[1]
    misfit = mine_ref[...].astype(f32) + other_ref[...].astype(f32) - goal_ref[...].astype(f32)
    loss = 0.5 * jnp.sum(misfit * misfit, keepdims=True)
    for ref in rest:
        loss = loss + jnp.sum(ref[...], keepdims=True)
    high = loss.astype(bf16).astype(f32)
    middle = (loss - high).astype(bf16).astype(f32)
    low = loss - high - middle
    lane = lax.broadcasted_iota(jnp.int32, (out_ref.shape[0], PAD), 1)
    tail = jnp.where(lane == 0, high, jnp.where(lane == 1, middle, jnp.where(lane == 2, low, 0.0)))
    out_ref[:, :width] = misfit.astype(bf16)
    out_ref[:, width:] = tail.astype(bf16)


def misfits(mine, other, goal, rest):
    rows, width = mine.shape
    operands = (mine, other, goal, *rest)
    return pl.pallas_call(
        misfit_kernel,
        out_shape=pltpu.VMEM((rows, width + PAD), bf16),
        in_specs=[VMEM_SPEC] * len(operands),
        out_specs=VMEM_SPEC,
        compiler_params=pltpu.CompilerParams(vmem_limit_bytes=8 << 20),
        cost_estimate=SHORT,
    )(*[in_vmem(x) for x in operands])


def loss_kernel(scale, *refs):
    pieces, out_ref = refs[:-1], refs[-1]
    total = jnp.zeros((1, 1), f32)
    for ref in pieces:
        tail = ref[:, ref.shape[1] - PAD :].astype(f32)
        total = total + jnp.sum(tail, keepdims=True)
    out_ref[...] = jnp.broadcast_to(total * scale, out_ref.shape)


def group_loss(pieces, block_rows):
    return pl.pallas_call(
        functools.partial(loss_kernel, 1.0 / block_rows),
        out_shape=pltpu.VMEM((8, PAD), f32),
        in_specs=[VMEM_SPEC] * len(pieces),
        out_specs=VMEM_SPEC,
        compiler_params=pltpu.CompilerParams(vmem_limit_bytes=8 << 20),
        cost_estimate=SHORT,
    )(*[in_vmem(x) for x in pieces])


def total_kernel(count, own_ref, *refs):
    total = functools.reduce(jnp.add, [ref[...] for ref in refs[:-1]], own_ref[...])
    refs[-1][...] = total[:1, :1] / count


def mean_loss(parts, count):
    return pl.pallas_call(
        functools.partial(total_kernel, count),
        out_shape=pltpu.VMEM((1, 1), f32),
        in_specs=[VMEM_SPEC] * len(parts),
        out_specs=VMEM_SPEC,
        compiler_params=pltpu.CompilerParams(vmem_limit_bytes=4 << 20),
        cost_estimate=SHORT,
    )(*[in_vmem(x) for x in parts])


def body(residual, targets, w_enc, b_enc, w_dec, block_mask):
    rows = residual.shape[1]
    width = residual.shape[2]
    layers = lax.axis_size("layer")
    feats = lax.axis_size("feat")
    tokens = rows * feats
    ring = Ring(feats)

    tokens_of = ring.owners[..., None] * rows + np.arange(rows)
    table = jnp.asarray((tokens_of // TBLOCK).reshape(feats, 1, -1).astype(np.float32))

    own = residual[0]
    twins = ring.across(own)
    held = {}

    def load_in(name, array, part, hop):
        def pin(ended):
            signal = ended[0][hop - 1] if hop else twins
            held[name, part] = loaded(array, part, signal)
            return [held[name, part]]

        return pin

    def rest_in(ended):
        held["decoder", 1], held["norm"], held["keep"] = prepared(
            block_mask[0], table, held["decoder", 0], w_dec[0], ended[1][ring.hops - 1]
        )
        return [held["decoder", 1], held["norm"], *held["keep"]]

    pins = {
        2: load_in("encoder", w_enc[0], 0, 0),
        3: load_in("encoder", w_enc[0], 1, 1),
        4: load_in("decoder", w_dec[0], 0, 2),
        0: rest_in,
    }
    gathered = gather(ring, own, twins, pins, True)
    encoder = [held["encoder", i] for i in (0, 1)]
    decoder = [held["decoder", i] for i in (0, 1)]

    acts, gates, sums, shares = zip(
        *[forward(ring, gathered[i], encoder, b_enc, held["keep"][i], decoder, i == 0) for i in (0, 1)]
    )
    act_sum = sums[0] + sums[1]

    def goals_in(ended):
        goal = after(targets[0], ended[0][0])
        goal = lax.ppermute(goal, "layer", [(i, (i - 1) % layers) for i in range(layers)])
        held["goal"] = [goal, ring.across(goal)]
        return list(held["goal"])

    def rest_in(ended):
        penalty = penalty_weight * act_sum * held["norm"]
        held["rest"] = [penalty, ring.across(penalty)]
        return held["rest"]

    pins = {4: lambda ended: goals_in(ended) + rest_in(ended)}
    summed = scatter_sums(ring, rows, shares, pins)
    payloads = [misfits(*summed[i], held["goal"][i], held["rest"][i : i + 1]) for i in (0, 1)]
    held["turned"] = []

    def rows_in(ended):
        chain = len(held["turned"])
        held["turned"].append(turned(after(gathered[chain], ended[1][chain])))
        return held["turned"][-1:]

    errors = gather(ring, *payloads, {3: rows_in, 4: rows_in}, False)
    group_losses = [group_loss([piece for parts in errors for piece in parts], rows)]
    for _ in range(layers - 1):
        route = [(i, (i + 1) % layers) for i in range(layers)]
        group_losses.append(lax.ppermute(group_losses[-1], "layer", route))
    enc_grad, bias_grad, dec_grad = backward(
        errors, list(acts), list(gates), held["turned"], decoder, held["norm"], act_sum
    )
    group_losses[0] = after(group_losses[0], bias_grad)
    loss = mean_loss(group_losses, layers * tokens * width).reshape(())
    return enc_grad[None], bias_grad, dec_grad[None], loss


def solution(mesh):
    return jax.shard_map(
        body,
        mesh=mesh,
        in_specs=(
            P("layer", "feat", None),
            P("layer", "feat", None),
            P("layer", None, "feat"),
            P("layer", "feat"),
            P("layer", "feat", None),
            P("layer", None, "feat"),
        ),
        out_specs=(P("layer", None, "feat"), P("layer", "feat"), P("layer", "feat", None), P()),
        check_vma=False,
    )
```

```python
import functools

import jax
import jax.numpy as jnp
import numpy as np
from jax import lax
from jax.experimental import pallas as pl
from jax.experimental.pallas import tpu as pltpu
from jax.sharding import PartitionSpec as P

TBLOCK = 128
FBLOCK = 128
PAD = 128

penalty_weight = 0.5
norm_epsilon = 1e-06
f32 = jnp.float32
bf16 = jnp.bfloat16


class Ring:
    def __init__(self, size):
        chips = size // 2
        self.hops = (chips - 1) // 2
        self.far = chips % 2 == 0
        order = list(range(0, chips, 2)) + list(range(1, chips, 2))[::-1]
        place = {chip: at for at, chip in enumerate(order)}
        self.step = []
        owners = []
        for device in range(size):
            chip, core = divmod(device, 2)
            at = place[chip]
            ahead = 1 if core == 0 else -1
            self.step.append((device, order[(at + ahead) % chips] * 2 + core))
            behind = [order[(at - ahead * k) % chips] for k in range(1, self.hops + 1)]
            front = [order[(at + ahead * k) % chips] for k in range(1, self.hops + 1)]
            last = [order[(at + self.hops + 1) % chips]] if self.far else []
            owners.append([[2 * c + i for c in [chip] + behind + front + last] for i in (core, 1 - core)])
        self.owners = np.array(owners, np.int32)
        self.twin = [(device, device ^ 1) for device in range(size)]

    def along(self, block):
        return lax.ppermute(block, "feat", self.step)

    def across(self, block):
        return lax.ppermute(block, "feat", self.twin)


def after(value, *signals):
    return lax.optimization_barrier((value, *signals))[0]


class Turns:
    def __init__(self, pins, leading):
        self.ended = [[], []]
        self.pins = pins
        self.leading = leading

    def enter(self, chain, block):
        hop = len(self.ended[chain])
        signals = self.ended[1 - chain][hop - 2 : hop - 1] if hop >= 2 else []
        if chain == self.leading and hop + 1 in self.pins:
            signals = signals + self.pins[hop + 1](self.ended)
        return after(block, *signals)

    def leave(self, chain, block):
        self.ended[chain].append(block)


def gather(ring, mine, twins, pins, direct):
    turns = Turns(pins, 0)
    moving = [mine, twins]
    front = [[], []]
    for k in range(ring.hops + ring.far):
        for chain in (0, 1):
            if k == ring.hops and chain == 1 and not direct:
                continue
            block = after(moving[chain], front[chain][k - 2]) if k >= 2 else moving[chain]
            moving[chain] = ring.along(turns.enter(chain, block))
            turns.leave(chain, moving[chain])
            if k < ring.hops and chain == 1:
                front[0].append(ring.across(after(turns.ended[0][k], moving[1])))
                front[1].append(ring.across(moving[1]))
    last = [[], []]
    if ring.far:
        last = [[moving[0]], [moving[1] if direct else ring.across(moving[0])]]
    parts = [
        [block] + turns.ended[chain][: ring.hops] + front[1 - chain] + last[chain]
        for chain, block in enumerate((mine, twins))
    ]
    if 0 in pins:
        parts = after(parts, *pins[0](turns.ended))
    return parts


def scatter_sums(ring, rows, shares, pins):
    turns = Turns(pins, 1)
    (own, sent, front, last), (own_twin, sent_twin, front_twin, _) = shares
    received = [ring.across(sent), ring.across(sent_twin)]
    arrived = [None, None]

    def send(chain, share, addend):
        total = share + addend.astype(f32)
        if arrived[chain] is not None:
            total = total + arrived[chain].astype(f32)
        arrived[chain] = ring.along(turns.enter(chain, total.astype(bf16)))
        turns.leave(chain, arrived[chain])

    def part(array, k):
        return array[rows * (k - 1) : rows * k]

    for k in range(ring.hops, -1, -1):
        if k > 0:
            send(0, part(front_twin, k), part(received[0], k))
        if k < ring.hops:
            send(1, part(front, k + 1), part(received[1], k + 1))
        elif ring.far:
            send(1, last, received[1][rows * ring.hops :])
    totals = []
    for share, came in ((own, arrived[1]), (own_twin, arrived[0])):
        totals.append((share if came is None else share + came.astype(f32)).astype(bf16))
    from_twin = [ring.across(total) for total in totals]
    return [(totals[0], from_twin[1]), (totals[1], from_twin[0])]


def in_vmem(x):
    return pltpu.with_memory_space_constraint(x, pltpu.VMEM)


def in_hbm(x):
    return pltpu.with_memory_space_constraint(x, pltpu.HBM)


VMEM_SPEC = pl.BlockSpec(memory_space=pltpu.VMEM)
ANY_SPEC = pl.BlockSpec(memory_space=pl.ANY)
HBM_SPEC = pl.BlockSpec(memory_space=pltpu.HBM)
SHORT = pl.CostEstimate(flops=0, bytes_accessed=0, transcendentals=0)
SMEM_SPEC = pl.BlockSpec(memory_space=pltpu.SMEM)


def stacked(refs, columns):
    return jnp.concatenate([ref[:, columns] for ref in refs], axis=0)


def whole_pieces(parts):
    if all(p.shape[0] % 16 == 0 for p in parts):
        return parts
    return [jnp.concatenate(parts, axis=0)]


def forward_kernel(count, step, *refs):
    pieces = refs[:count]
    enc_refs, dec_refs = refs[count : count + 2], refs[count + 2 : count + 4]
    bias_ref, keep_ref, act_ref, gate_ref, sum_ref = refs[count + 4 : count + 9]
    outs = refs[count + 9 :]
    width = dec_refs[0].shape[1]
    cut = width // 2
    preact = bias_ref[...]
    for i, enc_ref in enumerate(enc_refs):
        for at in range(0, cut, 512):
            preact = preact + jnp.dot(
                stacked(pieces, slice(i * cut + at, i * cut + at + 512)),
                enc_ref[at : at + 512, :],
                preferred_element_type=f32,
            )
    positive = jnp.maximum(preact, 0.0)
    keep = keep_ref[...]
    act = (keep * positive * positive).astype(bf16)
    act_ref[...] = act
    gate_ref[...] = keep * 2.0 * positive
    sum_ref[...] = jnp.sum(act.astype(f32), axis=0, keepdims=True)
    for at in range(0, width, step):
        columns = jnp.concatenate([ref[:, at : at + step] for ref in dec_refs], axis=0)
        part = jnp.dot(act, columns, preferred_element_type=f32)
        if len(outs) == 1:
            outs[0][:, at : at + step] = part
            continue
        own_ref, sent_ref, front_ref = outs[:3]
        rows, hop = own_ref.shape[0], front_ref.shape[0]
        own_ref[:, at : at + step] = part[:rows]
        sent_ref[:hop, at : at + step] = part[rows : rows + hop].astype(bf16)
        front_ref[:, at : at + step] = part[rows + hop : rows + 2 * hop]
        if len(outs) == 4:
            outs[3][:, at : at + step] = part[rows + 2 * hop :]
        else:
            sent_ref[hop:, at : at + step] = part[rows + 2 * hop :].astype(bf16)


def forward(ring, parts, encoder, bias, keep, decoder, keeps_last):
    pieces = whole_pieces(parts)
    rows, features = parts[0].shape[0], encoder[0].shape[1]
    total = sum(p.shape[0] for p in parts)
    hop = rows * ring.hops
    end = rows + 2 * hop
    width = decoder[0].shape[1]
    shapes = [((total, features), bf16), ((total, features), f32), ((1, features), f32)]
    apart = rows % 16 == 0 and ring.hops > 0 and ring.far
    if apart and keeps_last:
        shapes += [((rows, width), f32), ((hop, width), bf16), ((hop, width), f32), ((rows, width), f32)]
    elif apart:
        shapes += [((rows, width), f32), ((hop + rows, width), bf16), ((hop, width), f32)]
    else:
        shapes += [((total, width), f32)]
    outs = pl.pallas_call(
        functools.partial(forward_kernel, len(pieces), min(512, width)),
        out_shape=[pltpu.VMEM(shape, dtype) for shape, dtype in shapes],
        in_specs=[VMEM_SPEC] * (len(pieces) + 6),
        out_specs=[VMEM_SPEC] * len(shapes),
        compiler_params=pltpu.CompilerParams(vmem_limit_bytes=12 << 20),
        cost_estimate=SHORT,
    )(*[in_vmem(x) for x in (*pieces, *encoder, *decoder, bias, keep)])
    act, gate, act_sum = outs[:3]
    if apart:
        own, sent, front, *last = outs[3:]
        return act, gate, act_sum, (own, sent, front, last[0] if last else None)
    full = outs[3]
    sent = full[rows : rows + hop]
    if not keeps_last:
        sent = jnp.concatenate([sent, full[end:]], axis=0)
    return act, gate, act_sum, (full[:rows], sent.astype(bf16), full[rows + hop : end], full[end:])


def turn_kernel(*refs):
    pieces, out_ref = refs[:-1], refs[-1]
    step = 128 if out_ref.shape[0] % 128 == 0 else out_ref.shape[0]
    for at in range(0, out_ref.shape[0], step):
        out_ref[at : at + step, :] = stacked(pieces, slice(at, at + step)).T


def turned(parts):
    pieces = whole_pieces(parts)
    total = sum(p.shape[0] for p in pieces)
    width = pieces[0].shape[1]
    return pl.pallas_call(
        turn_kernel,
        out_shape=pltpu.VMEM((width, total), bf16),
        in_specs=[VMEM_SPEC] * len(pieces),
        out_specs=VMEM_SPEC,
        compiler_params=pltpu.CompilerParams(vmem_limit_bytes=12 << 20),
        cost_estimate=SHORT,
    )(*[in_vmem(x) for x in pieces])


def backward_kernel(counts, step, *refs):
    halves = len(counts)
    at = sum(counts)
    errors = refs[:at]
    acts, gates, rows = (refs[at + halves * i : at + halves * (i + 1)] for i in range(3))
    *dec_refs, norm_ref, sum_ref = refs[at + 3 * halves : at + 3 * halves + 4]
    enc_out, bias_out, dec_out = refs[at + 3 * halves + 4 : at + 3 * halves + 7]
    enc_stage, dec_stage, enc_sems, dec_sems = refs[at + 3 * halves + 7 :]
    features, width = dec_stage.shape
    turned_act = jnp.concatenate([a[...] for a in acts], axis=0).T
    coef = penalty_weight * sum_ref[...] / norm_ref[...]
    coef = jnp.broadcast_to(coef, (8, features)).T[:, :1]
    copies = []
    for i, at in enumerate(range(0, width, step)):
        columns = slice(at, at + step)
        grad = jnp.dot(turned_act, stacked(errors, columns), preferred_element_type=f32)
        grad = grad + coef * jnp.concatenate([ref[:, columns] for ref in dec_refs], axis=0).astype(f32)
        dec_stage[:, columns] = grad.astype(bf16)
        copy = pltpu.make_async_copy(dec_stage.at[:, columns], dec_out.at[:, columns], dec_sems.at[i])
        copy.start()
        copies.append(copy)
    total = turned_act.shape[1]
    act_grad = jnp.zeros((total, features), f32)
    for at in range(0, width, 512):
        columns = slice(at, at + 512)
        act_grad = act_grad + lax.dot_general(
            stacked(errors, columns), stacked(dec_refs, columns), (((1,), (1,)), ((), ())), preferred_element_type=f32
        )
    gate = jnp.concatenate([g[...] for g in gates], axis=0)
    pre_grad = ((act_grad + penalty_weight * norm_ref[...]) * gate).astype(bf16)
    bias_out[...] = jnp.sum(pre_grad.astype(f32), axis=0, keepdims=True)
    for i, at in enumerate(range(0, width, step)):
        here = slice(at, at + step)
        left = jnp.concatenate([r[here, :] for r in rows], axis=1)
        enc_stage[here, :] = jnp.dot(left, pre_grad, preferred_element_type=f32).astype(bf16)
        copy = pltpu.make_async_copy(enc_stage.at[here, :], enc_out.at[here, :], enc_sems.at[i])
        copy.start()
        copies.append(copy)
    for copy in copies:
        copy.wait()


def backward(errors, acts, gates, rows, decoder, norms, act_sum):
    errors = [whole_pieces(e) for e in errors]
    features, width = sum(d.shape[0] for d in decoder), decoder[0].shape[1]
    step = min(512, width)
    operands = [x for e in errors for x in e] + acts + gates + rows + [*decoder, norms, act_sum]
    total = sum(a.shape[0] for a in acts)
    return pl.pallas_call(
        functools.partial(backward_kernel, tuple(len(e) for e in errors), step),
        out_shape=[
            jax.ShapeDtypeStruct((width, features), bf16),
            jax.ShapeDtypeStruct((1, features), f32),
            jax.ShapeDtypeStruct((features, width), bf16),
        ],
        in_specs=[VMEM_SPEC] * len(operands),
        out_specs=[ANY_SPEC, VMEM_SPEC, ANY_SPEC],
        scratch_shapes=[
            pltpu.VMEM((width, features), bf16),
            pltpu.VMEM((features, width), bf16),
            pltpu.SemaphoreType.DMA((width // step,)),
            pltpu.SemaphoreType.DMA((width // step,)),
        ],
        compiler_params=pltpu.CompilerParams(vmem_limit_bytes=24 << 20),
        cost_estimate=SHORT,
    )(*[in_vmem(x) for x in operands])


def load_kernel(first, source_ref, signal_ref, out_ref, sems):
    pieces = sems.shape[0]
    rows = out_ref.shape[0] // pieces
    copies = []
    for i in range(pieces):
        copy = pltpu.make_async_copy(
            source_ref.at[first + i * rows : first + (i + 1) * rows], out_ref.at[i * rows : (i + 1) * rows], sems.at[i]
        )
        copy.start()
        copies.append(copy)
    for copy in copies:
        copy.wait()


def loaded(array, part, signal):
    rows = array.shape[0] // 2
    return pl.pallas_call(
        functools.partial(load_kernel, part * rows),
        out_shape=pltpu.VMEM((rows, array.shape[1]), array.dtype),
        in_specs=[HBM_SPEC, VMEM_SPEC],
        out_specs=VMEM_SPEC,
        scratch_shapes=[pltpu.SemaphoreType.DMA((4,))],
        compiler_params=pltpu.CompilerParams(vmem_limit_bytes=4 << 20),
        cost_estimate=SHORT,
    )(in_hbm(array), in_vmem(signal))


def prepare_kernel(mask_ref, table_ref, half_ref, source_ref, signal_ref, dec_ref, norm_ref, *rest):
    keep_refs, (row_ref, row_sem, sems) = rest[:-3], rest[-3:]
    row = pltpu.make_async_copy(table_ref.at[lax.axis_index("feat")], row_ref, row_sem)
    row.start()
    pieces = sems.shape[0]
    rows, width = dec_ref.shape[0] // pieces, dec_ref.shape[1]
    copies = []
    for i in range(pieces):
        here = slice(i * rows, (i + 1) * rows)
        there = slice(dec_ref.shape[0] + i * rows, dec_ref.shape[0] + (i + 1) * rows)
        copy = pltpu.make_async_copy(source_ref.at[there], dec_ref.at[here], sems.at[i])
        copy.start()
        copies.append(copy)
    row.wait()
    token_block = jnp.broadcast_to(row_ref[...], (8, row_ref.shape[1])).T[:, :1]
    for i, out_ref in enumerate(keep_refs):
        total = out_ref.shape[0]
        here = token_block[i * total : (i + 1) * total]
        for j in range(mask_ref.shape[1]):
            column = jnp.zeros((total, FBLOCK), f32)
            for b in range(mask_ref.shape[0]):
                column = jnp.where(here == b, mask_ref[b, j].astype(f32), column)
            out_ref[:, j * FBLOCK : (j + 1) * FBLOCK] = column
    for half, ref in enumerate((half_ref, dec_ref)):
        for i in range(pieces):
            if half:
                copies[i].wait()
            here = slice(i * rows, (i + 1) * rows)
            partial = jnp.zeros((rows, 128), f32)
            for at in range(0, width, 128):
                part = ref[here, at : at + 128].astype(f32)
                partial = partial + part * part
            there = slice(half * dec_ref.shape[0] + i * rows, half * dec_ref.shape[0] + (i + 1) * rows)
            norm_ref[:, there] = jnp.sqrt(jnp.sum(partial.T, axis=0, keepdims=True) + norm_epsilon)


def prepared(mask, table, half, decoder, signal):
    features = decoder.shape[0]
    total = table.shape[2] // 2
    dec, norm, *keep = pl.pallas_call(
        prepare_kernel,
        out_shape=[
            pltpu.VMEM(half.shape, half.dtype),
            pltpu.VMEM((1, features), f32),
            pltpu.VMEM((total, features), f32),
            pltpu.VMEM((total, features), f32),
        ],
        in_specs=[SMEM_SPEC, HBM_SPEC, VMEM_SPEC, HBM_SPEC, VMEM_SPEC],
        out_specs=[VMEM_SPEC] * 4,
        scratch_shapes=[
            pltpu.VMEM((1, table.shape[2]), f32),
            pltpu.SemaphoreType.DMA,
            pltpu.SemaphoreType.DMA((max(1, half.shape[0] // 128),)),
        ],
        compiler_params=pltpu.CompilerParams(vmem_limit_bytes=4 << 20),
        cost_estimate=SHORT,
    )(mask, in_hbm(table), in_vmem(half), in_hbm(decoder), in_vmem(signal))
    return dec, norm, keep


def misfit_kernel(*refs):
    mine_ref, other_ref, goal_ref = refs[:3]
    rest, out_ref = refs[3:-1], refs[-1]
    width = mine_ref.shape[1]
    misfit = mine_ref[...].astype(f32) + other_ref[...].astype(f32) - goal_ref[...].astype(f32)
    loss = 0.5 * jnp.sum(misfit * misfit, keepdims=True)
    for ref in rest:
        loss = loss + jnp.sum(ref[...], keepdims=True)
    high = loss.astype(bf16).astype(f32)
    middle = (loss - high).astype(bf16).astype(f32)
    low = loss - high - middle
    lane = lax.broadcasted_iota(jnp.int32, (out_ref.shape[0], PAD), 1)
    tail = jnp.where(lane == 0, high, jnp.where(lane == 1, middle, jnp.where(lane == 2, low, 0.0)))
    out_ref[:, :width] = misfit.astype(bf16)
    out_ref[:, width:] = tail.astype(bf16)


def misfits(mine, other, goal, rest):
    rows, width = mine.shape
    operands = (mine, other, goal, *rest)
    return pl.pallas_call(
        misfit_kernel,
        out_shape=pltpu.VMEM((rows, width + PAD), bf16),
        in_specs=[VMEM_SPEC] * len(operands),
        out_specs=VMEM_SPEC,
        compiler_params=pltpu.CompilerParams(vmem_limit_bytes=8 << 20),
        cost_estimate=SHORT,
    )(*[in_vmem(x) for x in operands])


def loss_kernel(scale, *refs):
    pieces, out_ref = refs[:-1], refs[-1]
    total = jnp.zeros((1, 1), f32)
    for ref in pieces:
        tail = ref[:, ref.shape[1] - PAD :].astype(f32)
        total = total + jnp.sum(tail, keepdims=True)
    out_ref[...] = jnp.broadcast_to(total * scale, out_ref.shape)


def group_loss(pieces, block_rows):
    return pl.pallas_call(
        functools.partial(loss_kernel, 1.0 / block_rows),
        out_shape=pltpu.VMEM((8, PAD), f32),
        in_specs=[VMEM_SPEC] * len(pieces),
        out_specs=VMEM_SPEC,
        compiler_params=pltpu.CompilerParams(vmem_limit_bytes=8 << 20),
        cost_estimate=SHORT,
    )(*[in_vmem(x) for x in pieces])


def total_kernel(count, own_ref, *refs):
    total = functools.reduce(jnp.add, [ref[...] for ref in refs[:-1]], own_ref[...])
    refs[-1][...] = total[:1, :1] / count


def mean_loss(parts, count):
    return pl.pallas_call(
        functools.partial(total_kernel, count),
        out_shape=pltpu.VMEM((1, 1), f32),
        in_specs=[VMEM_SPEC] * len(parts),
        out_specs=VMEM_SPEC,
        compiler_params=pltpu.CompilerParams(vmem_limit_bytes=4 << 20),
        cost_estimate=SHORT,
    )(*[in_vmem(x) for x in parts])


def body(residual, targets, w_enc, b_enc, w_dec, block_mask):
    rows = residual.shape[1]
    width = residual.shape[2]
    layers = lax.axis_size("layer")
    feats = lax.axis_size("feat")
    tokens = rows * feats
    ring = Ring(feats)

    tokens_of = ring.owners[..., None] * rows + np.arange(rows)
    table = jnp.asarray((tokens_of // TBLOCK).reshape(feats, 1, -1).astype(np.float32))

    own = residual[0]
    twins = ring.across(own)
    held = {}

    def load_in(name, array, part, hop):
        def pin(ended):
            signal = ended[0][hop - 1] if hop else twins
            held[name, part] = loaded(array, part, signal)
            return [held[name, part]]

        return pin

    def rest_in(ended):
        held["decoder", 1], held["norm"], held["keep"] = prepared(
            block_mask[0], table, held["decoder", 0], w_dec[0], ended[1][ring.hops - 1]
        )
        return [held["decoder", 1], held["norm"], *held["keep"]]

    pins = {
        2: load_in("encoder", w_enc[0], 0, 0),
        3: load_in("encoder", w_enc[0], 1, 1),
        4: load_in("decoder", w_dec[0], 0, 2),
        0: rest_in,
    }
    gathered = gather(ring, own, twins, pins, True)
    encoder = [held["encoder", i] for i in (0, 1)]
    decoder = [held["decoder", i] for i in (0, 1)]

    acts, gates, sums, shares = zip(
        *[forward(ring, gathered[i], encoder, b_enc, held["keep"][i], decoder, i == 0) for i in (0, 1)]
    )
    act_sum = sums[0] + sums[1]

    def goals_in(ended):
        goal = after(targets[0], ended[0][0])
        goal = lax.ppermute(goal, "layer", [(i, (i - 1) % layers) for i in range(layers)])
        held["goal"] = [goal, ring.across(goal)]
        return list(held["goal"])

    def rest_in(ended):
        penalty = penalty_weight * act_sum * held["norm"]
        held["rest"] = [penalty, ring.across(penalty)]
        return held["rest"]

    pins = {4: lambda ended: goals_in(ended) + rest_in(ended)}
    summed = scatter_sums(ring, rows, shares, pins)
    payloads = [misfits(*summed[i], held["goal"][i], held["rest"][i : i + 1]) for i in (0, 1)]
    held["turned"] = []

    def rows_in(ended):
        chain = len(held["turned"])
        held["turned"].append(turned(after(gathered[chain], ended[1][chain])))
        return held["turned"][-1:]

    errors = gather(ring, *payloads, {3: rows_in, 4: rows_in}, False)
    group_losses = [group_loss([piece for parts in errors for piece in parts], rows)]
    for _ in range(layers - 1):
        route = [(i, (i + 1) % layers) for i in range(layers)]
        group_losses.append(lax.ppermute(group_losses[-1], "layer", route))
    enc_grad, bias_grad, dec_grad = backward(
        errors, list(acts), list(gates), held["turned"], decoder, held["norm"], act_sum
    )
    group_losses[0] = after(group_losses[0], bias_grad)
    loss = mean_loss(group_losses, layers * tokens * width).reshape(())
    return enc_grad[None], bias_grad, dec_grad[None], loss


def solution(mesh):
    return jax.shard_map(
        body,
        mesh=mesh,
        in_specs=(
            P("layer", "feat", None),
            P("layer", "feat", None),
            P("layer", None, "feat"),
            P("layer", "feat"),
            P("layer", "feat", None),
            P("layer", None, "feat"),
        ),
        out_specs=(P("layer", None, "feat"), P("layer", "feat"), P("layer", "feat", None), P()),
        check_vma=False,
    )
```

```python
import functools

import jax
import jax.numpy as jnp
import numpy as np
from jax import lax
from jax.experimental import pallas as pl
from jax.experimental.pallas import tpu as pltpu
from jax.sharding import PartitionSpec as P

TBLOCK = 128
FBLOCK = 128
PAD = 128

penalty_weight = 0.5
norm_epsilon = 1e-06
f32 = jnp.float32
bf16 = jnp.bfloat16


class Ring:
    def __init__(self, size):
        chips = size // 2
        self.hops = (chips - 1) // 2
        self.far = chips % 2 == 0
        order = list(range(0, chips, 2)) + list(range(1, chips, 2))[::-1]
        place = {chip: at for at, chip in enumerate(order)}
        self.step = []
        owners = []
        for device in range(size):
            chip, core = divmod(device, 2)
            at = place[chip]
            ahead = 1 if core == 0 else -1
            self.step.append((device, order[(at + ahead) % chips] * 2 + core))
            behind = [order[(at - ahead * k) % chips] for k in range(1, self.hops + 1)]
            front = [order[(at + ahead * k) % chips] for k in range(1, self.hops + 1)]
            last = [order[(at + self.hops + 1) % chips]] if self.far else []
            owners.append([[2 * c + i for c in [chip] + behind + front + last] for i in (core, 1 - core)])
        self.owners = np.array(owners, np.int32)
        self.twin = [(device, device ^ 1) for device in range(size)]

    def along(self, block):
        return lax.ppermute(block, "feat", self.step)

    def across(self, block):
        return lax.ppermute(block, "feat", self.twin)


def after(value, *signals):
    return lax.optimization_barrier((value, *signals))[0]


class Turns:
    def __init__(self, pins, leading):
        self.ended = [[], []]
        self.pins = pins
        self.leading = leading

    def enter(self, chain, block):
        hop = len(self.ended[chain])
        signals = self.ended[1 - chain][hop - 2 : hop - 1] if hop >= 2 else []
        if chain == self.leading and hop + 1 in self.pins:
            signals = signals + self.pins[hop + 1](self.ended)
        return after(block, *signals)

    def leave(self, chain, block):
        self.ended[chain].append(block)


def gather(ring, mine, twins, pins, direct):
    turns = Turns(pins, 0)
    moving = [mine, twins]
    front = [[], []]
    for k in range(ring.hops + ring.far):
        for chain in (0, 1):
            if k == ring.hops and chain == 1 and not direct:
                continue
            block = after(moving[chain], front[chain][k - 2]) if k >= 2 else moving[chain]
            moving[chain] = ring.along(turns.enter(chain, block))
            turns.leave(chain, moving[chain])
            if k < ring.hops and chain == 1:
                front[0].append(ring.across(after(turns.ended[0][k], moving[1])))
                front[1].append(ring.across(moving[1]))
    last = [[], []]
    if ring.far:
        last = [[moving[0]], [moving[1] if direct else ring.across(moving[0])]]
    parts = [
        [block] + turns.ended[chain][: ring.hops] + front[1 - chain] + last[chain]
        for chain, block in enumerate((mine, twins))
    ]
    if 0 in pins:
        parts = after(parts, *pins[0](turns.ended))
    return parts


def scatter_sums(ring, rows, shares, pins):
    turns = Turns(pins, 1)
    (own, sent, front, last), (own_twin, sent_twin, front_twin, _) = shares
    received = [ring.across(sent), ring.across(sent_twin)]
    arrived = [None, None]

    def send(chain, share, addend):
        total = share + addend.astype(f32)
        if arrived[chain] is not None:
            total = total + arrived[chain].astype(f32)
        arrived[chain] = ring.along(turns.enter(chain, total.astype(bf16)))
        turns.leave(chain, arrived[chain])

    def part(array, k):
        return array[rows * (k - 1) : rows * k]

    for k in range(ring.hops, -1, -1):
        if k > 0:
            send(0, part(front_twin, k), part(received[0], k))
        if k < ring.hops:
            send(1, part(front, k + 1), part(received[1], k + 1))
        elif ring.far:
            send(1, last, received[1][rows * ring.hops :])
    totals = []
    for share, came in ((own, arrived[1]), (own_twin, arrived[0])):
        totals.append((share if came is None else share + came.astype(f32)).astype(bf16))
    from_twin = [ring.across(total) for total in totals]
    return [(totals[0], from_twin[1]), (totals[1], from_twin[0])]


def in_vmem(x):
    return pltpu.with_memory_space_constraint(x, pltpu.VMEM)


def in_hbm(x):
    return pltpu.with_memory_space_constraint(x, pltpu.HBM)


VMEM_SPEC = pl.BlockSpec(memory_space=pltpu.VMEM)
ANY_SPEC = pl.BlockSpec(memory_space=pl.ANY)
HBM_SPEC = pl.BlockSpec(memory_space=pltpu.HBM)
SHORT = pl.CostEstimate(flops=0, bytes_accessed=0, transcendentals=0)
SMEM_SPEC = pl.BlockSpec(memory_space=pltpu.SMEM)


def stacked(refs, columns):
    return jnp.concatenate([ref[:, columns] for ref in refs], axis=0)


def whole_pieces(parts):
    if all(p.shape[0] % 16 == 0 for p in parts):
        return parts
    return [jnp.concatenate(parts, axis=0)]


def forward_kernel(count, step, *refs):
    pieces = refs[:count]
    enc_refs, dec_refs = refs[count : count + 1], refs[count + 1 : count + 3]
    bias_ref, keep_ref, act_ref, gate_ref, sum_ref = refs[count + 3 : count + 8]
    outs = refs[count + 8 :]
    width = dec_refs[0].shape[1]
    cut = width
    preact = bias_ref[...]
    for i, enc_ref in enumerate(enc_refs):
        for at in range(0, cut, 512):
            preact = preact + jnp.dot(
                stacked(pieces, slice(i * cut + at, i * cut + at + 512)),
                enc_ref[at : at + 512, :],
                preferred_element_type=f32,
            )
    positive = jnp.maximum(preact, 0.0)
    keep = keep_ref[...]
    act = (keep * positive * positive).astype(bf16)
    act_ref[...] = act
    gate_ref[...] = keep * 2.0 * positive
    sum_ref[...] = jnp.sum(act.astype(f32), axis=0, keepdims=True)
    for at in range(0, width, step):
        columns = jnp.concatenate([ref[:, at : at + step] for ref in dec_refs], axis=0)
        part = jnp.dot(act, columns, preferred_element_type=f32)
        if len(outs) == 1:
            outs[0][:, at : at + step] = part
            continue
        own_ref, sent_ref, front_ref = outs[:3]
        rows, hop = own_ref.shape[0], front_ref.shape[0]
        own_ref[:, at : at + step] = part[:rows]
        sent_ref[:hop, at : at + step] = part[rows : rows + hop].astype(bf16)
        front_ref[:, at : at + step] = part[rows + hop : rows + 2 * hop]
        if len(outs) == 4:
            outs[3][:, at : at + step] = part[rows + 2 * hop :]
        else:
            sent_ref[hop:, at : at + step] = part[rows + 2 * hop :].astype(bf16)


def forward(ring, parts, encoder, bias, keep, decoder, keeps_last):
    pieces = whole_pieces(parts)
    rows, features = parts[0].shape[0], encoder[0].shape[1]
    total = sum(p.shape[0] for p in parts)
    hop = rows * ring.hops
    end = rows + 2 * hop
    width = decoder[0].shape[1]
    shapes = [((total, features), bf16), ((total, features), f32), ((1, features), f32)]
    apart = rows % 16 == 0 and ring.hops > 0 and ring.far
    if apart and keeps_last:
        shapes += [((rows, width), f32), ((hop, width), bf16), ((hop, width), f32), ((rows, width), f32)]
    elif apart:
        shapes += [((rows, width), f32), ((hop + rows, width), bf16), ((hop, width), f32)]
    else:
        shapes += [((total, width), f32)]
    outs = pl.pallas_call(
        functools.partial(forward_kernel, len(pieces), min(512, width)),
        out_shape=[pltpu.VMEM(shape, dtype) for shape, dtype in shapes],
        in_specs=[VMEM_SPEC] * (len(pieces) + 5),
        out_specs=[VMEM_SPEC] * len(shapes),
        compiler_params=pltpu.CompilerParams(vmem_limit_bytes=12 << 20),
        cost_estimate=SHORT,
    )(*[in_vmem(x) for x in (*pieces, *encoder, *decoder, bias, keep)])
    act, gate, act_sum = outs[:3]
    if apart:
        own, sent, front, *last = outs[3:]
        return act, gate, act_sum, (own, sent, front, last[0] if last else None)
    full = outs[3]
    sent = full[rows : rows + hop]
    if not keeps_last:
        sent = jnp.concatenate([sent, full[end:]], axis=0)
    return act, gate, act_sum, (full[:rows], sent.astype(bf16), full[rows + hop : end], full[end:])


def turn_kernel(*refs):
    pieces, out_ref = refs[:-1], refs[-1]
    step = 128 if out_ref.shape[0] % 128 == 0 else out_ref.shape[0]
    for at in range(0, out_ref.shape[0], step):
        out_ref[at : at + step, :] = stacked(pieces, slice(at, at + step)).T


def turned(parts):
    pieces = whole_pieces(parts)
    total = sum(p.shape[0] for p in pieces)
    width = pieces[0].shape[1]
    return pl.pallas_call(
        turn_kernel,
        out_shape=pltpu.VMEM((width, total), bf16),
        in_specs=[VMEM_SPEC] * len(pieces),
        out_specs=VMEM_SPEC,
        compiler_params=pltpu.CompilerParams(vmem_limit_bytes=12 << 20),
        cost_estimate=SHORT,
    )(*[in_vmem(x) for x in pieces])


def backward_kernel(counts, step, *refs):
    halves = len(counts)
    at = sum(counts)
    errors = refs[:at]
    acts, gates, rows = (refs[at + halves * i : at + halves * (i + 1)] for i in range(3))
    *dec_refs, norm_ref, sum_ref = refs[at + 3 * halves : at + 3 * halves + 4]
    enc_out, bias_out, dec_out = refs[at + 3 * halves + 4 : at + 3 * halves + 7]
    enc_stage, dec_stage, enc_sems, dec_sems = refs[at + 3 * halves + 7 :]
    features, width = dec_stage.shape
    turned_act = jnp.concatenate([a[...] for a in acts], axis=0).T
    coef = penalty_weight * sum_ref[...] / norm_ref[...]
    coef = jnp.broadcast_to(coef, (8, features)).T[:, :1]
    copies = []
    for i, at in enumerate(range(0, width, step)):
        columns = slice(at, at + step)
        grad = jnp.dot(turned_act, stacked(errors, columns), preferred_element_type=f32)
        grad = grad + coef * jnp.concatenate([ref[:, columns] for ref in dec_refs], axis=0).astype(f32)
        dec_stage[:, columns] = grad.astype(bf16)
        copy = pltpu.make_async_copy(dec_stage.at[:, columns], dec_out.at[:, columns], dec_sems.at[i])
        copy.start()
        copies.append(copy)
    total = turned_act.shape[1]
    act_grad = jnp.zeros((total, features), f32)
    for at in range(0, width, 512):
        columns = slice(at, at + 512)
        act_grad = act_grad + lax.dot_general(
            stacked(errors, columns), stacked(dec_refs, columns), (((1,), (1,)), ((), ())), preferred_element_type=f32
        )
    gate = jnp.concatenate([g[...] for g in gates], axis=0)
    pre_grad = ((act_grad + penalty_weight * norm_ref[...]) * gate).astype(bf16)
    bias_out[...] = jnp.sum(pre_grad.astype(f32), axis=0, keepdims=True)
    for i, at in enumerate(range(0, width, step)):
        here = slice(at, at + step)
        left = jnp.concatenate([r[here, :] for r in rows], axis=1)
        enc_stage[here, :] = jnp.dot(left, pre_grad, preferred_element_type=f32).astype(bf16)
        copy = pltpu.make_async_copy(enc_stage.at[here, :], enc_out.at[here, :], enc_sems.at[i])
        copy.start()
        copies.append(copy)
    for copy in copies:
        copy.wait()


def backward(errors, acts, gates, rows, decoder, norms, act_sum):
    errors = [whole_pieces(e) for e in errors]
    features, width = sum(d.shape[0] for d in decoder), decoder[0].shape[1]
    step = min(512, width)
    operands = [x for e in errors for x in e] + acts + gates + rows + [*decoder, norms, act_sum]
    total = sum(a.shape[0] for a in acts)
    return pl.pallas_call(
        functools.partial(backward_kernel, tuple(len(e) for e in errors), step),
        out_shape=[
            jax.ShapeDtypeStruct((width, features), bf16),
            jax.ShapeDtypeStruct((1, features), f32),
            jax.ShapeDtypeStruct((features, width), bf16),
        ],
        in_specs=[VMEM_SPEC] * len(operands),
        out_specs=[ANY_SPEC, VMEM_SPEC, ANY_SPEC],
        scratch_shapes=[
            pltpu.VMEM((width, features), bf16),
            pltpu.VMEM((features, width), bf16),
            pltpu.SemaphoreType.DMA((width // step,)),
            pltpu.SemaphoreType.DMA((width // step,)),
        ],
        compiler_params=pltpu.CompilerParams(vmem_limit_bytes=24 << 20),
        cost_estimate=SHORT,
    )(*[in_vmem(x) for x in operands])


def load_kernel(first, source_ref, signal_ref, out_ref, sems):
    pieces = sems.shape[0]
    rows = out_ref.shape[0] // pieces
    copies = []
    for i in range(pieces):
        copy = pltpu.make_async_copy(
            source_ref.at[first + i * rows : first + (i + 1) * rows], out_ref.at[i * rows : (i + 1) * rows], sems.at[i]
        )
        copy.start()
        copies.append(copy)
    for copy in copies:
        copy.wait()


def loaded(array, part, signal):
    rows = array.shape[0] // 2
    return pl.pallas_call(
        functools.partial(load_kernel, part * rows),
        out_shape=pltpu.VMEM((rows, array.shape[1]), array.dtype),
        in_specs=[HBM_SPEC, VMEM_SPEC],
        out_specs=VMEM_SPEC,
        scratch_shapes=[pltpu.SemaphoreType.DMA((4,))],
        compiler_params=pltpu.CompilerParams(vmem_limit_bytes=4 << 20),
        cost_estimate=SHORT,
    )(in_hbm(array), in_vmem(signal))


def prepare_kernel(mask_ref, table_ref, half_ref, source_ref, signal_ref, dec_ref, norm_ref, *rest):
    keep_refs, (row_ref, row_sem, sems) = rest[:-3], rest[-3:]
    row = pltpu.make_async_copy(table_ref.at[lax.axis_index("feat")], row_ref, row_sem)
    row.start()
    pieces = sems.shape[0]
    rows, width = dec_ref.shape[0] // pieces, dec_ref.shape[1]
    copies = []
    for i in range(pieces):
        here = slice(i * rows, (i + 1) * rows)
        there = slice(dec_ref.shape[0] + i * rows, dec_ref.shape[0] + (i + 1) * rows)
        copy = pltpu.make_async_copy(source_ref.at[there], dec_ref.at[here], sems.at[i])
        copy.start()
        copies.append(copy)
    row.wait()
    token_block = jnp.broadcast_to(row_ref[...], (8, row_ref.shape[1])).T[:, :1]
    for i, out_ref in enumerate(keep_refs):
        total = out_ref.shape[0]
        here = token_block[i * total : (i + 1) * total]
        for j in range(mask_ref.shape[1]):
            column = jnp.zeros((total, FBLOCK), f32)
            for b in range(mask_ref.shape[0]):
                column = jnp.where(here == b, mask_ref[b, j].astype(f32), column)
            out_ref[:, j * FBLOCK : (j + 1) * FBLOCK] = column
    for half, ref in enumerate((half_ref, dec_ref)):
        for i in range(pieces):
            if half:
                copies[i].wait()
            here = slice(i * rows, (i + 1) * rows)
            partial = jnp.zeros((rows, 128), f32)
            for at in range(0, width, 128):
                part = ref[here, at : at + 128].astype(f32)
                partial = partial + part * part
            there = slice(half * dec_ref.shape[0] + i * rows, half * dec_ref.shape[0] + (i + 1) * rows)
            norm_ref[:, there] = jnp.sqrt(jnp.sum(partial.T, axis=0, keepdims=True) + norm_epsilon)


def prepared(mask, table, half, decoder, signal):
    features = decoder.shape[0]
    total = table.shape[2] // 2
    dec, norm, *keep = pl.pallas_call(
        prepare_kernel,
        out_shape=[
            pltpu.VMEM(half.shape, half.dtype),
            pltpu.VMEM((1, features), f32),
            pltpu.VMEM((total, features), f32),
            pltpu.VMEM((total, features), f32),
        ],
        in_specs=[SMEM_SPEC, HBM_SPEC, VMEM_SPEC, HBM_SPEC, VMEM_SPEC],
        out_specs=[VMEM_SPEC] * 4,
        scratch_shapes=[
            pltpu.VMEM((1, table.shape[2]), f32),
            pltpu.SemaphoreType.DMA,
            pltpu.SemaphoreType.DMA((max(1, half.shape[0] // 128),)),
        ],
        compiler_params=pltpu.CompilerParams(vmem_limit_bytes=4 << 20),
        cost_estimate=SHORT,
    )(mask, in_hbm(table), in_vmem(half), in_hbm(decoder), in_vmem(signal))
    return dec, norm, keep


def misfit_kernel(*refs):
    mine_ref, other_ref, goal_ref = refs[:3]
    rest, out_ref = refs[3:-1], refs[-1]
    width = mine_ref.shape[1]
    misfit = mine_ref[...].astype(f32) + other_ref[...].astype(f32) - goal_ref[...].astype(f32)
    loss = 0.5 * jnp.sum(misfit * misfit, keepdims=True)
    for ref in rest:
        loss = loss + jnp.sum(ref[...], keepdims=True)
    high = loss.astype(bf16).astype(f32)
    middle = (loss - high).astype(bf16).astype(f32)
    low = loss - high - middle
    lane = lax.broadcasted_iota(jnp.int32, (out_ref.shape[0], PAD), 1)
    tail = jnp.where(lane == 0, high, jnp.where(lane == 1, middle, jnp.where(lane == 2, low, 0.0)))
    out_ref[:, :width] = misfit.astype(bf16)
    out_ref[:, width:] = tail.astype(bf16)


def misfits(mine, other, goal, rest):
    rows, width = mine.shape
    operands = (mine, other, goal, *rest)
    return pl.pallas_call(
        misfit_kernel,
        out_shape=pltpu.VMEM((rows, width + PAD), bf16),
        in_specs=[VMEM_SPEC] * len(operands),
        out_specs=VMEM_SPEC,
        compiler_params=pltpu.CompilerParams(vmem_limit_bytes=8 << 20),
        cost_estimate=SHORT,
    )(*[in_vmem(x) for x in operands])


def loss_kernel(scale, *refs):
    pieces, out_ref = refs[:-1], refs[-1]
    total = jnp.zeros((1, 1), f32)
    for ref in pieces:
        tail = ref[:, ref.shape[1] - PAD :].astype(f32)
        total = total + jnp.sum(tail, keepdims=True)
    out_ref[...] = jnp.broadcast_to(total * scale, out_ref.shape)


def group_loss(pieces, block_rows):
    return pl.pallas_call(
        functools.partial(loss_kernel, 1.0 / block_rows),
        out_shape=pltpu.VMEM((8, PAD), f32),
        in_specs=[VMEM_SPEC] * len(pieces),
        out_specs=VMEM_SPEC,
        compiler_params=pltpu.CompilerParams(vmem_limit_bytes=8 << 20),
        cost_estimate=SHORT,
    )(*[in_vmem(x) for x in pieces])


def total_kernel(count, own_ref, *refs):
    total = functools.reduce(jnp.add, [ref[...] for ref in refs[:-1]], own_ref[...])
    refs[-1][...] = total[:1, :1] / count


def mean_loss(parts, count):
    return pl.pallas_call(
        functools.partial(total_kernel, count),
        out_shape=pltpu.VMEM((1, 1), f32),
        in_specs=[VMEM_SPEC] * len(parts),
        out_specs=VMEM_SPEC,
        compiler_params=pltpu.CompilerParams(vmem_limit_bytes=4 << 20),
        cost_estimate=SHORT,
    )(*[in_vmem(x) for x in parts])


def body(residual, targets, w_enc, b_enc, w_dec, block_mask):
    rows = residual.shape[1]
    width = residual.shape[2]
    layers = lax.axis_size("layer")
    feats = lax.axis_size("feat")
    tokens = rows * feats
    ring = Ring(feats)

    tokens_of = ring.owners[..., None] * rows + np.arange(rows)
    table = jnp.asarray((tokens_of // TBLOCK).reshape(feats, 1, -1).astype(np.float32))

    own = residual[0]
    twins = ring.across(own)
    held = {}

    def load_in(name, array, part, hop):
        def pin(ended):
            signal = ended[0][hop - 1] if hop else twins
            held[name, part] = loaded(array, part, signal)
            return [held[name, part]]

        return pin

    def rest_in(ended):
        held["decoder", 1], held["norm"], held["keep"] = prepared(
            block_mask[0], table, held["decoder", 0], w_dec[0], ended[1][ring.hops - 1]
        )
        return [held["decoder", 1], held["norm"], *held["keep"]]

    pins = {4: load_in("decoder", w_dec[0], 0, 2), 0: rest_in}
    gathered = gather(ring, own, twins, pins, True)
    encoder = [w_enc[0]]
    decoder = [held["decoder", i] for i in (0, 1)]

    acts, gates, sums, shares = zip(
        *[forward(ring, gathered[i], encoder, b_enc, held["keep"][i], decoder, i == 0) for i in (0, 1)]
    )
    act_sum = sums[0] + sums[1]

    def goals_in(ended):
        goal = after(targets[0], ended[0][0])
        goal = lax.ppermute(goal, "layer", [(i, (i - 1) % layers) for i in range(layers)])
        held["goal"] = [goal, ring.across(goal)]
        return list(held["goal"])

    def rest_in(ended):
        penalty = penalty_weight * act_sum * held["norm"]
        held["rest"] = [penalty, ring.across(penalty)]
        return held["rest"]

    pins = {4: lambda ended: goals_in(ended) + rest_in(ended)}
    summed = scatter_sums(ring, rows, shares, pins)
    payloads = [misfits(*summed[i], held["goal"][i], held["rest"][i : i + 1]) for i in (0, 1)]
    held["turned"] = []

    def rows_in(ended):
        chain = len(held["turned"])
        held["turned"].append(turned(after(gathered[chain], ended[1][chain])))
        return held["turned"][-1:]

    errors = gather(ring, *payloads, {3: rows_in, 4: rows_in}, False)
    group_losses = [group_loss([piece for parts in errors for piece in parts], rows)]
    for _ in range(layers - 1):
        route = [(i, (i + 1) % layers) for i in range(layers)]
        group_losses.append(lax.ppermute(group_losses[-1], "layer", route))
    enc_grad, bias_grad, dec_grad = backward(
        errors, list(acts), list(gates), held["turned"], decoder, held["norm"], act_sum
    )
    group_losses[0] = after(group_losses[0], bias_grad)
    loss = mean_loss(group_losses, layers * tokens * width).reshape(())
    return enc_grad[None], bias_grad, dec_grad[None], loss


def solution(mesh):
    return jax.shard_map(
        body,
        mesh=mesh,
        in_specs=(
            P("layer", "feat", None),
            P("layer", "feat", None),
            P("layer", None, "feat"),
            P("layer", "feat"),
            P("layer", "feat", None),
            P("layer", None, "feat"),
        ),
        out_specs=(P("layer", None, "feat"), P("layer", "feat"), P("layer", "feat", None), P()),
        check_vma=False,
    )
```
